32 devices in a mesh: dp: 16 (over z, y, core), tensor: 2 (over x).
Axes of the slice: x: 2, y: 2, z: 4, core: 2. Of those that a mesh axis runs over, the one named last changes fastest.
Arguments:
- tokens: bfloat16 [8192, 3072], P('dp', 'tensor'), may hold values from -6 to 6
- w_in: bfloat16 [3072, 3072], P('dp', 'tensor'), may hold values from -0.109375 to 0.109375
- cotangent: bfloat16 [8192, 3072], P('dp', 'tensor'), may hold values from -6 to 6
Outputs:
- hidden: bfloat16 [8192, 3072], P('dp', 'tensor')
- x_grad: bfloat16 [8192, 3072], P('dp', 'tensor')
- w_grad: bfloat16 [3072, 3072], P('dp', 'tensor')
The draws below stay inside these ranges and needn't reach their ends.
All inputs are finite; a program needn't handle non-finite values.
Results may differ from the reference program's by a relative error of at most 0.028.
Values may be sent and summed in bfloat16 or wider, within the bound.
A program may use at most 128 MiB of HBM per device.

```python
import jax
import jax.numpy as jnp
from jax import lax

D = 3072
FF_DEV = 1536
TOK_DEV = 512
FF = 3072
TOKENS = 8192
N_DP = 16
N_TENSOR = 2


def with_spikes(array, stream_key, source, target, parts, factor):
    def block_of(position):
        return (jnp.arange(array.shape[position]) // (array.shape[position] // parts)).reshape((-1,) + (1,) * (array.ndim - 1 - position))

    first = jax.random.permutation(stream_key, parts)[block_of(target)]
    second = (block_of(target) + parts // 2) % parts
    return jnp.where((block_of(source) == first) | (block_of(source) == second), factor * array, array)


def level_of(key, shape, split, low, high):
    loudness = 1.0
    for position, blocks in split:
        steps = jax.random.uniform(jax.random.fold_in(jax.random.fold_in(key, 6), position), (blocks,), jnp.float32, low / len(split), high / len(split))
        loudness = loudness * jnp.repeat(jnp.exp(steps), shape[position] // blocks).reshape((-1,) + (1,) * (len(shape) - 1 - position))
    return loudness


def normal_values(stream_key, shape, spread, most, pieces=(), kind=jnp.bfloat16):
    entries = spread * jax.random.normal(stream_key, shape, jnp.float32)
    if pieces:
        entries = entries * level_of(stream_key, shape, pieces, -0.22, 0.18)
    return jnp.clip(entries, -most, most).astype(kind)


def noise_with(key, extent, scale, limit, pieces, heavy, kind=jnp.bfloat16):
    entries = scale * jax.random.normal(key, extent, jnp.float32)
    if pieces:
        entries = entries * level_of(key, extent, pieces, -0.22, 0.18)
    return jnp.clip(with_spikes(entries, jax.random.fold_in(key, 3), *heavy), -limit, limit).astype(kind)


def setup_inputs(seed: int = 0) -> dict:
    streams_of = jax.random.split(jax.random.key(seed), 4)
    tokens = noise_with(streams_of[0], (TOKENS, D), 1.0, 6.0, ((0, 16), (1, 2)), (0, 1, 16, 2.0))
    w_in = normal_values(streams_of[1], (D, FF), D ** -0.5, 0.109375, ((0, 16), (1, 2)))
    cotangent = normal_values(streams_of[2], (TOKENS, FF), 1.0, 6.0, ((0, 16), (1, 2)))
    return dict(tokens=tokens, w_in=w_in, cotangent=cotangent)


def gelu_tanh(values):
    return jax.nn.gelu(values, approximate=True)

def reference(tokens, w_in, cotangent):
    row_groups = tokens.reshape(N_DP, TOK_DEV, D)
    cot_groups = cotangent.reshape(N_DP, TOK_DEV, FF)

    def accumulate(running, pair):
        row_block, cot_block = pair
        preact = jnp.dot(row_block, w_in, preferred_element_type=jnp.float32)
        activ, pull_back = jax.vjp(gelu_tanh, preact)
        pre_grad = pull_back(cot_block.astype(jnp.float32))[0].astype(jnp.bfloat16)
        input_grad = jnp.zeros((TOK_DEV, D), jnp.float32)
        for group in range(N_TENSOR):
            grad_cols = pre_grad[:, group * FF_DEV:(group + 1) * FF_DEV]
            weight_cols = w_in[:, group * FF_DEV:(group + 1) * FF_DEV]
            piece = lax.dot_general(grad_cols, weight_cols, (((1,), (1,)), ((), ())), preferred_element_type=jnp.float32)
            piece = lax.optimization_barrier(piece.astype(jnp.bfloat16)).astype(jnp.float32)
            input_grad = input_grad + piece
        partial_value = lax.dot_general(row_block, pre_grad, (((0,), (0,)), ((), ())), preferred_element_type=jnp.float32)
        partial_value = lax.optimization_barrier(partial_value.astype(jnp.bfloat16)).astype(jnp.float32)
        return (running + partial_value, (activ.astype(jnp.bfloat16), input_grad.astype(jnp.bfloat16)))
    start = jnp.zeros((D, FF), jnp.float32)
    summed, (hidden, x_grad) = lax.scan(accumulate, start, (row_groups, cot_groups))
    return (hidden.reshape(TOKENS, FF), x_grad.reshape(TOKENS, D), summed.astype(jnp.bfloat16))
```

```python
import functools

import jax
import jax.numpy as jnp
from jax import lax
from jax.experimental import pallas as pl
from jax.experimental.pallas import tpu as pltpu
from jax.sharding import PartitionSpec as P

BF16 = jnp.bfloat16
F32 = jnp.float32
GROUPS = 2
DIRS = 2
TILE = 256
RS_LAG = 2
ROOT = 0.7978845608028654


def kernel(
    n, peers, w_hbm, tok_hbm, cot_hbm, hid, xg, wg,
    w_all, tok, tok_t, cot, pg, part, psend, precv, rsend, rrecv, xsend, xrecv,
    load_sem, tok_s, tok_r, ag_s, ag_r, agp_s, agp_r,
    rs_s, rs_r, rsp_s, rsp_r, x_s, x_r,
):
    S = w_hbm.shape[0]
    rows, dx = tok_hbm.shape
    ff = cot_hbm.shape[1]
    gcols = ff // GROUPS
    qcols = gcols // DIRS
    xcols = xsend.shape[2]
    nb = dx // xcols
    halves = rows // TILE
    ntile = gcols // TILE
    units = halves * ntile
    ag_lag = n // 2

    dp = lax.axis_index("dp")
    x = lax.axis_index("tensor")
    c = lax.rem(dp, 2)
    q = lax.div(dp, 2)
    odd = lax.rem(q, 2)
    p = (1 - odd) * lax.div(q, 2) + odd * (n - lax.div(q + 1, 2))

    def chip_at(pos):
        pos = lax.rem(pos + 2 * n, n)
        far = lax.div(pos, n // 2)
        return (1 - far) * 2 * pos + far * (2 * n - 1 - 2 * pos)

    ring_to = [{"dp": chip_at(p + 1) * 2 + c}, {"dp": chip_at(p - 1) * 2 + c}]
    mate = {"dp": q * 2 + 1 - c}

    def peer(t):
        return {"tensor": lax.rem(x + t, peers)}

    w_load = pltpu.make_async_copy(
        w_hbm, w_all.at[pl.ds(pl.multiple_of(dp * S, 16), S), :], load_sem.at[0])
    tok_load = pltpu.make_async_copy(
        tok_hbm, tok.at[:, pl.ds(pl.multiple_of(x * dx, 128), dx)], load_sem.at[1])
    cot_load = pltpu.make_async_copy(cot_hbm, cot, load_sem.at[2])
    w_load.start()
    tok_load.start()
    cot_load.start()

    barrier = pltpu.get_barrier_semaphore()
    for who in ring_to + [mate] + [peer(t) for t in range(1, peers)]:
        pl.semaphore_signal(
            barrier, inc=1, device_id=who, device_id_type=pl.DeviceIdType.MESH)
    pl.semaphore_wait(barrier, 3 + peers - 1)

    def remote(src, dst, ssem, rsem, who):
        return pltpu.make_async_remote_copy(
            src_ref=src, dst_ref=dst, send_sem=ssem, recv_sem=rsem,
            device_id=who, device_id_type=pl.DeviceIdType.MESH)

    def w_piece(g, d, pos):
        owner = chip_at(pos) * 2 + c
        return w_all.at[pl.ds(pl.multiple_of(owner * S, 16), S),
                        pl.ds(g * gcols + d * qcols, qcols)]

    def w_piece_mate(g, d, pos):
        owner = chip_at(pos) * 2 + 1 - c
        return w_all.at[pl.ds(pl.multiple_of(owner * S, 16), S),
                        pl.ds(g * gcols + d * qcols, qcols)]

    def sign(d):
        return 1 - 2 * d

    def ag_ring(g, d, h):
        piece = w_piece(g, d, p - sign(d) * h)
        k = (g * DIRS + d) * n + h
        return remote(piece, piece, ag_s.at[k], ag_r.at[k], ring_to[d])

    def ag_ring_in(g, d, h):
        piece = w_piece(g, d, p - sign(d) * (h + 1))
        k = (g * DIRS + d) * n + h
        return remote(piece, piece, ag_s.at[k], ag_r.at[k], ring_to[d])

    def ag_mate(g, d, h):
        piece = w_piece(g, d, p - sign(d) * h)
        k = (g * DIRS + d) * n + h
        return remote(piece, piece, agp_s.at[k], agp_r.at[k], mate)

    def ag_mate_in(g, d, h):
        piece = w_piece_mate(g, d, p - sign(d) * h)
        k = (g * DIRS + d) * n + h
        return remote(piece, piece, agp_s.at[k], agp_r.at[k], mate)

    def tok_copy(t, m):
        piece = tok.at[pl.ds(m * TILE, TILE), pl.ds(pl.multiple_of(x * dx, 128), dx)]
        k = (t - 1) * halves + m
        return remote(piece, piece, tok_s.at[k], tok_r.at[k], peer(t))

    def tok_in(t, m):
        source = lax.rem(x + peers - t, peers)
        piece = tok.at[pl.ds(m * TILE, TILE), pl.ds(pl.multiple_of(source * dx, 128), dx)]
        k = (t - 1) * halves + m
        return remote(piece, piece, tok_s.at[k], tok_r.at[k], peer(t))

    def ag_start(g):
        for d in range(DIRS):
            ag_ring(g, d, 0).start()
        for d in range(DIRS):
            ag_mate(g, d, 0).start()

    w_load.wait()
    ag_start(0)
    tok_load.wait()
    for m in range(halves):
        for t in range(1, peers):
            tok_copy(t, m).start()
    cot_load.wait()

    def wait_mates(g):
        @pl.loop(0, n)
        def _(h):
            for d in range(DIRS):
                ag_mate_in(g, d, h).wait_recv()

    def activate(g, u):
        m = lax.div(u, ntile)
        rsl = pl.ds(pl.multiple_of(m * TILE, TILE), TILE)
        csl = pl.ds(pl.multiple_of(g * gcols + lax.rem(u, ntile) * TILE, TILE), TILE)
        v = jnp.dot(tok[rsl, :], w_all[:, csl], preferred_element_type=F32)
        sq = v * v
        th = jnp.tanh(ROOT * v * (1.0 + 0.044715 * sq))
        half = 0.5 * (1.0 + th)
        hid[rsl, csl] = (v * half).astype(BF16)
        slope = half + 0.5 * v * (1.0 - th * th) * (ROOT * (1.0 + 3.0 * 0.044715 * sq))
        pg[rsl, csl] = (cot[rsl, csl].astype(F32) * slope).astype(BF16)

    @pl.loop(0, n - 1 + ag_lag)
    def _(s):
        for g in range(GROUPS):
            h = s - g * ag_lag

            @pl.when((h >= 0) & (h < n - 1))
            def _():
                for d in range(DIRS):
                    ag_ring_in(g, d, h).wait_recv()

                    @pl.when(h < n - 2)
                    def _():
                        ag_ring(g, d, h + 1).start()

                    ag_mate(g, d, h + 1).start()

        @pl.when(s == ag_lag - 1)
        def _():
            ag_start(1)

        @pl.when(s == n - 1)
        def _():
            wait_mates(0)

        late = s - (n - 1)

        @pl.when(late >= 0)
        def _():
            @pl.loop(lax.div(late * units, ag_lag), lax.div((late + 1) * units, ag_lag))
            def _(u):
                for m in range(halves):
                    @pl.when(u == m * ntile)
                    def _():
                        for t in range(1, peers):
                            tok_in(t, m).wait_recv()

                        @pl.loop(0, tok.shape[1] // TILE)
                        def _(k):
                            at = pl.ds(pl.multiple_of(k * TILE, TILE), TILE)
                            tok_t[at, m * TILE:(m + 1) * TILE] = (
                                tok[m * TILE:(m + 1) * TILE, at].T)

                activate(0, u)

    def rs_owner(d, h):
        return chip_at(p - sign(d) * (h + 1))

    def slot(g, d, h):
        return (g * DIRS + d) * n + h

    def rs_ring(g, d, h):
        k = slot(g, d, h)
        return remote(rsend.at[k], rrecv.at[k], rs_s.at[k], rs_r.at[k], ring_to[d])

    def rs_mate(g, d, h):
        k = slot(g, d, h)
        return remote(psend.at[k], precv.at[k], rsp_s.at[k], rsp_r.at[k], mate)

    def make_part(g, d, h):
        cols = g * gcols + d * qcols
        acc = part.at[g * DIRS + d]
        acc[...] = jnp.dot(
            tok_t[pl.ds(pl.multiple_of(rs_owner(d, h) * 2 * S, 16), 2 * S), :],
            pg[:, cols:cols + qcols], preferred_element_type=F32)
        psend[slot(g, d, h)] = acc[pl.ds(pl.multiple_of((1 - c) * S, 16), S), :].astype(BF16)
        rs_mate(g, d, h).start()

    def combine(g, d, h):
        k = slot(g, d, h)
        cols = g * gcols + d * qcols
        acc = part.at[g * DIRS + d]
        mine = pl.ds(pl.multiple_of(c * S, 16), S)
        rs_mate(g, d, h).wait_recv()

        @pl.when(h == 0)
        def _():
            rsend[k] = (acc[mine, :] + precv[k].astype(F32)).astype(BF16)

        @pl.when(h > 0)
        def _():
            rs_ring(g, d, h - 1).wait_recv()
            total = (acc[mine, :] + precv[k].astype(F32)
                     + rrecv[k - 1].astype(F32)).astype(BF16)

            @pl.when(h < n - 1)
            def _():
                rsend[k] = total

            @pl.when(h == n - 1)
            def _():
                wg[:, cols:cols + qcols] = total

        @pl.when(h < n - 1)
        def _():
            rs_ring(g, d, h).start()

    def x_block(owner, b):
        at = pl.ds(pl.multiple_of(owner * dx + b * xcols, 128), xcols)
        return lax.dot_general(
            pg[...], w_all[at, :], (((1,), (1,)), ((), ())),
            preferred_element_type=F32).astype(BF16)

    def x_copy(k):
        return remote(xsend.at[k], xrecv.at[k], x_s.at[k], x_r.at[k],
                      peer(lax.div(k, nb) + 1))

    away = (peers - 1) * nb

    @pl.loop(-1, n + RS_LAG)
    def _(s):
        for g in range(GROUPS):
            h = s - g * RS_LAG

            @pl.when((h >= 0) & (h < n))
            def _():
                for d in range(DIRS):
                    combine(g, d, h)

            if g == 1:
                @pl.when((s >= 0) & (s < RS_LAG))
                def _():
                    @pl.when(s == 0)
                    def _():
                        wait_mates(1)

                    @pl.loop(lax.div(s * units, RS_LAG), lax.div((s + 1) * units, RS_LAG))
                    def _(u):
                        activate(1, u)

            @pl.when((h >= -1) & (h < n - 1))
            def _():
                for d in range(DIRS):
                    make_part(g, d, h + 1)

        e = s - RS_LAG

        @pl.when((e >= 0) & (e < 2))
        def _():
            @pl.loop(lax.div(e * away, 2), lax.div((e + 1) * away, 2))
            def _(k):
                t = lax.div(k, nb) + 1
                xsend[k] = x_block(lax.rem(x + t, peers), lax.rem(k, nb))
                x_copy(k).start()

        @pl.when((e >= 2) & (e < 4))
        def _():
            @pl.loop(lax.div((e - 2) * nb, 2), lax.div((e - 1) * nb, 2))
            def _(b):
                xg[:, pl.ds(pl.multiple_of(b * xcols, 128), xcols)] = x_block(x, b)

    @pl.loop(0, nb)
    def _(b):
        at = pl.ds(pl.multiple_of(b * xcols, 128), xcols)
        total = xg[:, at].astype(F32)
        for t in range(1, peers):
            k = (t - 1) * nb + b
            x_copy(k).wait_recv()
            total = total + xrecv[k].astype(F32)
        xg[:, at] = total.astype(BF16)

    @pl.loop(0, n)
    def _(h):
        for g in range(GROUPS):
            for d in range(DIRS):
                ag_mate(g, d, h).wait_send()
                rs_mate(g, d, h).wait_send()

                @pl.when(h < n - 1)
                def _():
                    ag_ring(g, d, h).wait_send()
                    rs_ring(g, d, h).wait_send()

    @pl.loop(0, away)
    def _(k):
        x_copy(k).wait_send()

    for m in range(halves):
        for t in range(1, peers):
            tok_copy(t, m).wait_send()


def on_device(n_dp, peers, tokens, w_in, cotangent):
    n = n_dp // 2
    S, ff = w_in.shape
    rows, dx = tokens.shape
    D = dx * peers
    qcols = ff // (GROUPS * DIRS)
    xcols = min(384, dx)
    nx = (peers - 1) * (dx // xcols)
    slots = GROUPS * DIRS * n
    any_spec = pl.BlockSpec(memory_space=pl.ANY)
    vmem = pl.BlockSpec(memory_space=pltpu.VMEM)
    dma = pltpu.SemaphoreType.DMA
    halves = rows // TILE
    return pl.pallas_call(
        functools.partial(kernel, n, peers),
        out_shape=[
            jax.ShapeDtypeStruct((rows, ff), BF16),
            jax.ShapeDtypeStruct((rows, dx), BF16),
            jax.ShapeDtypeStruct((S, ff), BF16),
        ],
        in_specs=[any_spec] * 3,
        out_specs=[vmem] * 3,
        scratch_shapes=[
            pltpu.VMEM((D, ff), BF16),
            pltpu.VMEM((rows, D), BF16),
            pltpu.VMEM((D, rows), BF16),
            pltpu.VMEM((rows, ff), BF16),
            pltpu.VMEM((rows, ff), BF16),
            pltpu.VMEM((GROUPS * DIRS, 2 * S, qcols), F32),
            pltpu.VMEM((slots, S, qcols), BF16),
            pltpu.VMEM((slots, S, qcols), BF16),
            pltpu.VMEM((slots, S, qcols), BF16),
            pltpu.VMEM((slots, S, qcols), BF16),
            pltpu.VMEM((nx, rows, xcols), BF16),
            pltpu.VMEM((nx, rows, xcols), BF16),
            dma((3,)),
            dma(((peers - 1) * halves,)), dma(((peers - 1) * halves,)),
            dma((slots,)), dma((slots,)), dma((slots,)), dma((slots,)),
            dma((slots,)), dma((slots,)), dma((slots,)), dma((slots,)),
            dma((nx,)), dma((nx,)),
        ],
        compiler_params=pltpu.CompilerParams(
            collective_id=0, has_side_effects=True,
            vmem_limit_bytes=60 * 1024 * 1024,
        ),
        cost_estimate=pl.CostEstimate(
            flops=6 * rows * D * ff, bytes_accessed=4 * (2 * rows * ff + rows * dx + S * ff),
            transcendentals=rows * ff),
    )(w_in, tokens, cotangent)


def solution(mesh):
    spec = P("dp", "tensor")
    return jax.shard_map(
        functools.partial(on_device, mesh.shape["dp"], mesh.shape["tensor"]),
        mesh=mesh, in_specs=(spec,) * 3, out_specs=(spec,) * 3, check_vma=False,
    )
```

```python
import functools

import jax
import jax.numpy as jnp
from jax import lax
from jax.experimental import pallas as pl
from jax.experimental.pallas import tpu as pltpu
from jax.sharding import PartitionSpec as P

BF16 = jnp.bfloat16
F32 = jnp.float32
GROUPS = 2
DIRS = 2
TILE = 256
SPLIT = 2
RS_LAG = 4
ROOT = 0.7978845608028654


def kernel(
    n, peers, w_hbm, tok_hbm, cot_hbm, hid, xg, wg,
    w_all, tok, tok_t, cot, pg, part, psend, precv, rsend, rrecv, xsend, xrecv,
    load_sem, tok_s, tok_r, ag_s, ag_r, agp_s, agp_r,
    rs_s, rs_r, rsp_s, rsp_r, x_s, x_r,
):
    S = w_hbm.shape[0]
    rows, dx = tok_hbm.shape
    ff = cot_hbm.shape[1]
    gcols = ff // GROUPS
    qcols = gcols // DIRS
    xcols = xsend.shape[2]
    nb = dx // xcols
    halves = rows // TILE
    ntile = gcols // TILE
    units = halves * ntile
    ag_lag = n // 2
    sr = S // SPLIT

    dp = lax.axis_index("dp")
    x = lax.axis_index("tensor")
    c = lax.rem(dp, 2)
    q = lax.div(dp, 2)
    odd = lax.rem(q, 2)
    p = (1 - odd) * lax.div(q, 2) + odd * (n - lax.div(q + 1, 2))

    def chip_at(pos):
        pos = lax.rem(pos + 2 * n, n)
        far = lax.div(pos, n // 2)
        return (1 - far) * 2 * pos + far * (2 * n - 1 - 2 * pos)

    ring_to = [{"dp": chip_at(p + 1) * 2 + c}, {"dp": chip_at(p - 1) * 2 + c}]
    mate = {"dp": q * 2 + 1 - c}

    def peer(t):
        return {"tensor": lax.rem(x + t, peers)}

    w_load = pltpu.make_async_copy(
        w_hbm, w_all.at[pl.ds(pl.multiple_of(dp * S, 16), S), :], load_sem.at[0])
    tok_load = pltpu.make_async_copy(
        tok_hbm, tok.at[:, pl.ds(pl.multiple_of(x * dx, 128), dx)], load_sem.at[1])
    cot_load = pltpu.make_async_copy(cot_hbm, cot, load_sem.at[2])
    w_load.start()
    tok_load.start()
    cot_load.start()

    barrier = pltpu.get_barrier_semaphore()
    for who in ring_to + [mate] + [peer(t) for t in range(1, peers)]:
        pl.semaphore_signal(
            barrier, inc=1, device_id=who, device_id_type=pl.DeviceIdType.MESH)
    pl.semaphore_wait(barrier, 3 + peers - 1)

    def remote(src, dst, ssem, rsem, who):
        return pltpu.make_async_remote_copy(
            src_ref=src, dst_ref=dst, send_sem=ssem, recv_sem=rsem,
            device_id=who, device_id_type=pl.DeviceIdType.MESH)

    def w_piece(g, d, pos, core, r):
        owner = chip_at(pos) * 2 + core
        return w_all.at[pl.ds(pl.multiple_of(owner * S + r * sr, 16), sr),
                        pl.ds(g * gcols + d * qcols, qcols)]

    def sem_at(g, d, h, r):
        return ((g * DIRS + d) * SPLIT + r) * n + h

    def sign(d):
        return 1 - 2 * d

    def ag_ring(g, d, h, r, back=0):
        piece = w_piece(g, d, p - sign(d) * (h + back), c, r)
        k = sem_at(g, d, h, r)
        return remote(piece, piece, ag_s.at[k], ag_r.at[k], ring_to[d])

    def ag_mate(g, d, h, r, core):
        piece = w_piece(g, d, p - sign(d) * h, core, r)
        k = sem_at(g, d, h, r)
        return remote(piece, piece, agp_s.at[k], agp_r.at[k], mate)

    def tok_copy(t, m):
        piece = tok.at[pl.ds(m * TILE, TILE), pl.ds(pl.multiple_of(x * dx, 128), dx)]
        k = (t - 1) * halves + m
        return remote(piece, piece, tok_s.at[k], tok_r.at[k], peer(t))

    def tok_in(t, m):
        source = lax.rem(x + peers - t, peers)
        piece = tok.at[pl.ds(m * TILE, TILE), pl.ds(pl.multiple_of(source * dx, 128), dx)]
        k = (t - 1) * halves + m
        return remote(piece, piece, tok_s.at[k], tok_r.at[k], peer(t))

    def ag_start(g):
        for r in range(SPLIT):
            for d in range(DIRS):
                ag_ring(g, d, 0, r).start()
        for r in range(SPLIT):
            for d in range(DIRS):
                ag_mate(g, d, 0, r, c).start()

    w_load.wait()
    ag_start(0)
    tok_load.wait()
    for m in range(halves):
        for t in range(1, peers):
            tok_copy(t, m).start()
    cot_load.wait()

    def wait_mates(g):
        @pl.loop(0, n)
        def _(h):
            for r in range(SPLIT):
                for d in range(DIRS):
                    ag_mate(g, d, h, r, 1 - c).wait_recv()

    def activate(g, u):
        m = lax.div(u, ntile)
        rsl = pl.ds(pl.multiple_of(m * TILE, TILE), TILE)
        csl = pl.ds(pl.multiple_of(g * gcols + lax.rem(u, ntile) * TILE, TILE), TILE)
        v = jnp.dot(tok[rsl, :], w_all[:, csl], preferred_element_type=F32)
        sq = v * v
        th = jnp.tanh(ROOT * v * (1.0 + 0.044715 * sq))
        half = 0.5 * (1.0 + th)
        hid[rsl, csl] = (v * half).astype(BF16)
        slope = half + 0.5 * v * (1.0 - th * th) * (ROOT * (1.0 + 3.0 * 0.044715 * sq))
        pg[rsl, csl] = (cot[rsl, csl].astype(F32) * slope).astype(BF16)

    def rs_owner(d, h):
        return chip_at(p - sign(d) * (h + 1))

    def slot(g, d, h):
        return (g * DIRS + d) * n + h

    def rs_ring(g, d, h, r):
        k = slot(g, d, h)
        at = pl.ds(r * sr, sr)
        j = sem_at(g, d, h, r)
        return remote(rsend.at[k, at], rrecv.at[k, at], rs_s.at[j], rs_r.at[j], ring_to[d])

    def rs_mate(g, d, h):
        k = slot(g, d, h)
        return remote(psend.at[k], precv.at[k], rsp_s.at[k], rsp_r.at[k], mate)

    def make_part(g, d, h):
        cols = g * gcols + d * qcols
        acc = part.at[g * DIRS + d]
        acc[...] = jnp.dot(
            tok_t[pl.ds(pl.multiple_of(rs_owner(d, h) * 2 * S, 16), 2 * S), :],
            pg[:, cols:cols + qcols], preferred_element_type=F32)
        psend[slot(g, d, h)] = acc[pl.ds(pl.multiple_of((1 - c) * S, 16), S), :].astype(BF16)
        rs_mate(g, d, h).start()

    def combine(g, h):
        for d in range(DIRS):
            rs_mate(g, d, h).wait_recv()
        for r in range(SPLIT):
            for d in range(DIRS):
                combine_piece(g, d, h, r)

    def combine_piece(g, d, h, r):
        k = slot(g, d, h)
        at = pl.ds(r * sr, sr)
        cols = g * gcols + d * qcols
        mine = part[g * DIRS + d, pl.ds(pl.multiple_of(c * S + r * sr, 16), sr), :]
        total = mine + precv[k, at].astype(F32)

        @pl.when(h == 0)
        def _():
            rsend[k, at] = total.astype(BF16)

        @pl.when(h > 0)
        def _():
            rs_ring(g, d, h - 1, r).wait_recv()
            full = (total + rrecv[k - 1, at].astype(F32)).astype(BF16)

            @pl.when(h < n - 1)
            def _():
                rsend[k, at] = full

            @pl.when(h == n - 1)
            def _():
                wg[at, cols:cols + qcols] = full

        @pl.when(h < n - 1)
        def _():
            rs_ring(g, d, h, r).start()

    @pl.loop(0, n - 1 + ag_lag)
    def _(s):
        late = s - (n - 1)

        @pl.when(late == ag_lag - 1)
        def _():
            for d in range(DIRS):
                make_part(0, d, 0)
            combine(0, 0)
            for d in range(DIRS):
                make_part(0, d, 1)

        for g in range(GROUPS):
            h = s - g * ag_lag

            @pl.when((h >= 0) & (h < n - 1))
            def _():
                for r in range(SPLIT):
                    for d in range(DIRS):
                        ag_ring(g, d, h, r, 1).wait_recv()

                        @pl.when(h < n - 2)
                        def _():
                            ag_ring(g, d, h + 1, r).start()

                        ag_mate(g, d, h + 1, r, c).start()

        @pl.when(s == ag_lag - 1)
        def _():
            ag_start(1)

        @pl.when(s == n - 1)
        def _():
            wait_mates(0)

        @pl.when((late >= 0) & (late < ag_lag - 1))
        def _():
            @pl.loop(lax.div(late * units, ag_lag - 1),
                     lax.div((late + 1) * units, ag_lag - 1))
            def _(u):
                for m in range(halves):
                    @pl.when(u == m * ntile)
                    def _():
                        for t in range(1, peers):
                            tok_in(t, m).wait_recv()

                        @pl.loop(0, tok.shape[1] // TILE)
                        def _(k):
                            at = pl.ds(pl.multiple_of(k * TILE, TILE), TILE)
                            tok_t[at, m * TILE:(m + 1) * TILE] = (
                                tok[m * TILE:(m + 1) * TILE, at].T)

                activate(0, u)

    def x_block(owner, b):
        at = pl.ds(pl.multiple_of(owner * dx + b * xcols, 128), xcols)
        return lax.dot_general(
            pg[...], w_all[at, :], (((1,), (1,)), ((), ())),
            preferred_element_type=F32).astype(BF16)

    def x_copy(k):
        return remote(xsend.at[k], xrecv.at[k], x_s.at[k], x_r.at[k],
                      peer(lax.div(k, nb) + 1))

    away = (peers - 1) * nb

    @pl.loop(1, n + RS_LAG)
    def _(s):
        for g in range(GROUPS):
            h = s - g * RS_LAG

            @pl.when((h >= 0) & (h < n))
            def _():
                combine(g, h)

            if g == 1:
                @pl.when(s < RS_LAG)
                def _():
                    @pl.when(s == 1)
                    def _():
                        wait_mates(1)

                    @pl.loop(lax.div((s - 1) * units, RS_LAG - 1),
                             lax.div(s * units, RS_LAG - 1))
                    def _(u):
                        activate(1, u)

            @pl.when((h >= -1) & (h < n - 1))
            def _():
                for d in range(DIRS):
                    make_part(g, d, h + 1)

        e = s - RS_LAG

        @pl.when((e >= 0) & (e < 2))
        def _():
            @pl.loop(lax.div(e * away, 2), lax.div((e + 1) * away, 2))
            def _(k):
                t = lax.div(k, nb) + 1
                xsend[k] = x_block(lax.rem(x + t, peers), lax.rem(k, nb))
                x_copy(k).start()

        @pl.when((e >= 2) & (e < 4))
        def _():
            @pl.loop(lax.div((e - 2) * nb, 2), lax.div((e - 1) * nb, 2))
            def _(b):
                xg[:, pl.ds(pl.multiple_of(b * xcols, 128), xcols)] = x_block(x, b)

    @pl.loop(0, nb)
    def _(b):
        at = pl.ds(pl.multiple_of(b * xcols, 128), xcols)
        total = xg[:, at].astype(F32)
        for t in range(1, peers):
            k = (t - 1) * nb + b
            x_copy(k).wait_recv()
            total = total + xrecv[k].astype(F32)
        xg[:, at] = total.astype(BF16)

    @pl.loop(0, n)
    def _(h):
        for g in range(GROUPS):
            for d in range(DIRS):
                rs_mate(g, d, h).wait_send()
                for r in range(SPLIT):
                    ag_mate(g, d, h, r, c).wait_send()

                    @pl.when(h < n - 1)
                    def _():
                        ag_ring(g, d, h, r).wait_send()
                        rs_ring(g, d, h, r).wait_send()

    @pl.loop(0, away)
    def _(k):
        x_copy(k).wait_send()

    for m in range(halves):
        for t in range(1, peers):
            tok_copy(t, m).wait_send()


def on_device(n_dp, peers, tokens, w_in, cotangent):
    n = n_dp // 2
    S, ff = w_in.shape
    rows, dx = tokens.shape
    D = dx * peers
    qcols = ff // (GROUPS * DIRS)
    xcols = min(384, dx)
    nx = (peers - 1) * (dx // xcols)
    slots = GROUPS * DIRS * n
    any_spec = pl.BlockSpec(memory_space=pl.ANY)
    vmem = pl.BlockSpec(memory_space=pltpu.VMEM)
    dma = pltpu.SemaphoreType.DMA
    halves = rows // TILE
    return pl.pallas_call(
        functools.partial(kernel, n, peers),
        out_shape=[
            jax.ShapeDtypeStruct((rows, ff), BF16),
            jax.ShapeDtypeStruct((rows, dx), BF16),
            jax.ShapeDtypeStruct((S, ff), BF16),
        ],
        in_specs=[any_spec] * 3,
        out_specs=[vmem] * 3,
        scratch_shapes=[
            pltpu.VMEM((D, ff), BF16),
            pltpu.VMEM((rows, D), BF16),
            pltpu.VMEM((D, rows), BF16),
            pltpu.VMEM((rows, ff), BF16),
            pltpu.VMEM((rows, ff), BF16),
            pltpu.VMEM((GROUPS * DIRS, 2 * S, qcols), F32),
            pltpu.VMEM((slots, S, qcols), BF16),
            pltpu.VMEM((slots, S, qcols), BF16),
            pltpu.VMEM((slots, S, qcols), BF16),
            pltpu.VMEM((slots, S, qcols), BF16),
            pltpu.VMEM((nx, rows, xcols), BF16),
            pltpu.VMEM((nx, rows, xcols), BF16),
            dma((3,)),
            dma(((peers - 1) * halves,)), dma(((peers - 1) * halves,)),
            dma((slots * SPLIT,)), dma((slots * SPLIT,)),
            dma((slots * SPLIT,)), dma((slots * SPLIT,)),
            dma((slots * SPLIT,)), dma((slots * SPLIT,)), dma((slots,)), dma((slots,)),
            dma((nx,)), dma((nx,)),
        ],
        compiler_params=pltpu.CompilerParams(
            collective_id=0, has_side_effects=True,
            vmem_limit_bytes=60 * 1024 * 1024,
        ),
        cost_estimate=pl.CostEstimate(
            flops=6 * rows * D * ff, bytes_accessed=4 * (2 * rows * ff + rows * dx + S * ff),
            transcendentals=rows * ff),
    )(w_in, tokens, cotangent)


def solution(mesh):
    spec = P("dp", "tensor")
    return jax.shard_map(
        functools.partial(on_device, mesh.shape["dp"], mesh.shape["tensor"]),
        mesh=mesh, in_specs=(spec,) * 3, out_specs=(spec,) * 3, check_vma=False,
    )
```

```python
import functools

import jax
import jax.numpy as jnp
from jax import lax
from jax.experimental import pallas as pl
from jax.experimental.pallas import tpu as pltpu
from jax.sharding import PartitionSpec as P

BF16 = jnp.bfloat16
F32 = jnp.float32
GROUPS = 3
DIRS = 2
TILE = 256
SPLIT = 2
RS_LAG = 3
ROOT = 0.7978845608028654


def kernel(
    n, peers, w_hbm, tok_hbm, cot_hbm, hid, xg, wg,
    w_all, tok, tok_t, cot, pg, part, psend, precv, rsend, rrecv, xsend, xrecv,
    load_sem, tok_s, tok_r, ag_s, ag_r, agp_s, agp_r,
    rs_s, rs_r, rsp_s, rsp_r, x_s, x_r,
):
    S = w_hbm.shape[0]
    rows, dx = tok_hbm.shape
    ff = cot_hbm.shape[1]
    gcols = ff // GROUPS
    qcols = gcols // DIRS
    xcols = xsend.shape[2]
    nb = dx // xcols
    halves = rows // TILE
    ntile = gcols // TILE
    units = halves * ntile
    ag_lag = max(2, 3 * n // 8)
    last = 2 * ag_lag - 1
    sr = S // SPLIT

    dp = lax.axis_index("dp")
    x = lax.axis_index("tensor")
    c = lax.rem(dp, 2)
    q = lax.div(dp, 2)
    odd = lax.rem(q, 2)
    p = (1 - odd) * lax.div(q, 2) + odd * (n - lax.div(q + 1, 2))

    def chip_at(pos):
        pos = lax.rem(pos + 2 * n, n)
        far = lax.div(pos, n // 2)
        return (1 - far) * 2 * pos + far * (2 * n - 1 - 2 * pos)

    ring_to = [{"dp": chip_at(p + 1) * 2 + c}, {"dp": chip_at(p - 1) * 2 + c}]
    mate = {"dp": q * 2 + 1 - c}

    def peer(t):
        return {"tensor": lax.rem(x + t, peers)}

    w_load = pltpu.make_async_copy(
        w_hbm, w_all.at[pl.ds(pl.multiple_of(dp * S, 16), S), :], load_sem.at[0])
    tok_load = pltpu.make_async_copy(
        tok_hbm, tok.at[:, pl.ds(pl.multiple_of(x * dx, 128), dx)], load_sem.at[1])
    cot_load = pltpu.make_async_copy(cot_hbm, cot, load_sem.at[2])
    w_load.start()
    tok_load.start()
    cot_load.start()

    barrier = pltpu.get_barrier_semaphore()
    for who in ring_to + [mate] + [peer(t) for t in range(1, peers)]:
        pl.semaphore_signal(
            barrier, inc=1, device_id=who, device_id_type=pl.DeviceIdType.MESH)
    pl.semaphore_wait(barrier, 3 + peers - 1)

    def remote(src, dst, ssem, rsem, who):
        return pltpu.make_async_remote_copy(
            src_ref=src, dst_ref=dst, send_sem=ssem, recv_sem=rsem,
            device_id=who, device_id_type=pl.DeviceIdType.MESH)

    def w_piece(g, d, pos, core, r):
        owner = chip_at(pos) * 2 + core
        return w_all.at[pl.ds(pl.multiple_of(owner * S + r * sr, 16), sr),
                        pl.ds(g * gcols + d * qcols, qcols)]

    def sem_at(g, d, h, r):
        return ((g * DIRS + d) * SPLIT + r) * n + h

    def sign(d):
        return 1 - 2 * d

    def ag_ring(g, d, h, r, back=0):
        piece = w_piece(g, d, p - sign(d) * (h + back), c, r)
        k = sem_at(g, d, h, r)
        return remote(piece, piece, ag_s.at[k], ag_r.at[k], ring_to[d])

    def ag_mate(g, d, h, r, core):
        piece = w_piece(g, d, p - sign(d) * h, core, r)
        k = sem_at(g, d, h, r)
        return remote(piece, piece, agp_s.at[k], agp_r.at[k], mate)

    def tok_copy(t, m):
        piece = tok.at[pl.ds(m * TILE, TILE), pl.ds(pl.multiple_of(x * dx, 128), dx)]
        k = (t - 1) * halves + m
        return remote(piece, piece, tok_s.at[k], tok_r.at[k], peer(t))

    def tok_in(t, m):
        source = lax.rem(x + peers - t, peers)
        piece = tok.at[pl.ds(m * TILE, TILE), pl.ds(pl.multiple_of(source * dx, 128), dx)]
        k = (t - 1) * halves + m
        return remote(piece, piece, tok_s.at[k], tok_r.at[k], peer(t))

    def ag_start(g):
        for r in range(SPLIT):
            for d in range(DIRS):
                ag_ring(g, d, 0, r).start()
        for r in range(SPLIT):
            for d in range(DIRS):
                ag_mate(g, d, 0, r, c).start()

    w_load.wait()
    ag_start(0)
    tok_load.wait()
    for m in range(halves):
        for t in range(1, peers):
            tok_copy(t, m).start()
    cot_load.wait()

    def wait_mates(g):
        @pl.loop(0, n)
        def _(h):
            for r in range(SPLIT):
                for d in range(DIRS):
                    ag_mate(g, d, h, r, 1 - c).wait_recv()

    def activate(g, u):
        m = lax.div(u, ntile)
        rsl = pl.ds(pl.multiple_of(m * TILE, TILE), TILE)
        csl = pl.ds(pl.multiple_of(g * gcols + lax.rem(u, ntile) * TILE, TILE), TILE)
        v = jnp.dot(tok[rsl, :], w_all[:, csl], preferred_element_type=F32)
        sq = v * v
        th = jnp.tanh(ROOT * v * (1.0 + 0.044715 * sq))
        half = 0.5 * (1.0 + th)
        hid[rsl, csl] = (v * half).astype(BF16)
        slope = half + 0.5 * v * (1.0 - th * th) * (ROOT * (1.0 + 3.0 * 0.044715 * sq))
        pg[rsl, csl] = (cot[rsl, csl].astype(F32) * slope).astype(BF16)

    def rs_owner(d, h):
        return chip_at(p - sign(d) * (h + 1))

    def slot(g, d, h):
        return (g * DIRS + d) * n + h

    def rs_ring(g, d, h, r):
        k = slot(g, d, h)
        at = pl.ds(r * sr, sr)
        j = sem_at(g, d, h, r)
        return remote(rsend.at[k, at], rrecv.at[k, at], rs_s.at[j], rs_r.at[j], ring_to[d])

    def rs_mate(g, d, h):
        k = slot(g, d, h)
        return remote(psend.at[k], precv.at[k], rsp_s.at[k], rsp_r.at[k], mate)

    def make_part(g, d, h):
        cols = g * gcols + d * qcols
        acc = part.at[g * DIRS + d]
        acc[...] = jnp.dot(
            tok_t[pl.ds(pl.multiple_of(rs_owner(d, h) * 2 * S, 16), 2 * S), :],
            pg[:, cols:cols + qcols], preferred_element_type=F32)
        psend[slot(g, d, h)] = acc[pl.ds(pl.multiple_of((1 - c) * S, 16), S), :].astype(BF16)
        rs_mate(g, d, h).start()

    def combine(g, h):
        for d in range(DIRS):
            rs_mate(g, d, h).wait_recv()
        for r in range(SPLIT):
            for d in range(DIRS):
                combine_piece(g, d, h, r)

    def combine_piece(g, d, h, r):
        k = slot(g, d, h)
        at = pl.ds(r * sr, sr)
        cols = g * gcols + d * qcols
        mine = part[g * DIRS + d, pl.ds(pl.multiple_of(c * S + r * sr, 16), sr), :]
        total = mine + precv[k, at].astype(F32)

        @pl.when(h == 0)
        def _():
            rsend[k, at] = total.astype(BF16)

        @pl.when(h > 0)
        def _():
            rs_ring(g, d, h - 1, r).wait_recv()
            full = (total + rrecv[k - 1, at].astype(F32)).astype(BF16)

            @pl.when(h < n - 1)
            def _():
                rsend[k, at] = full

            @pl.when(h == n - 1)
            def _():
                wg[at, cols:cols + qcols] = full

        @pl.when(h < n - 1)
        def _():
            rs_ring(g, d, h, r).start()

    strips = dx // 128
    others = (peers - 1) * strips

    def spread(count, i, steps):
        return lax.div(i * count, steps), lax.div((i + 1) * count, steps)

    def flip(m, col):
        at = pl.ds(pl.multiple_of(col, 128), 128)
        tok_t[at, m * TILE:(m + 1) * TILE] = tok[m * TILE:(m + 1) * TILE, at].T

    def flip_other(m, k):
        t = lax.div(k, strips) + 1
        flip(m, lax.rem(x + t, peers) * dx + lax.rem(k, strips) * 128)

    def await_tokens(m):
        for t in range(1, peers):
            tok_in(t, m).wait_recv()

    @pl.loop(0, n - 1 + 2 * ag_lag)
    def _(s):
        late = s - (n - 1)

        @pl.when(late == last)
        def _():
            for d in range(DIRS):
                make_part(0, d, 0)
            combine(0, 0)
            for d in range(DIRS):
                make_part(0, d, 1)

        for g in range(GROUPS):
            h = s - g * ag_lag

            @pl.when((h >= 0) & (h < n - 1))
            def _():
                for r in range(SPLIT):
                    for d in range(DIRS):
                        ag_ring(g, d, h, r, 1).wait_recv()

                        @pl.when(h < n - 2)
                        def _():
                            ag_ring(g, d, h + 1, r).start()

                        ag_mate(g, d, h + 1, r, c).start()

            if g + 1 < GROUPS:
                @pl.when(h == ag_lag - 1)
                def _():
                    ag_start(g + 1)

        @pl.when(late < 0)
        def _():
            @pl.loop(*spread(strips, s, n - 1))
            def _(k):
                for m in range(halves):
                    flip(m, x * dx + k * 128)

        @pl.when(late == 0)
        def _():
            wait_mates(0)
            await_tokens(0)

        @pl.when((late >= 0) & (late < ag_lag))
        def _():
            @pl.loop(*spread(units, late, ag_lag))
            def _(u):
                @pl.when(u == ntile)
                def _():
                    await_tokens(1)

                activate(0, u)

            @pl.loop(*spread(others, late, ag_lag))
            def _(k):
                flip_other(0, k)

        @pl.when(late == ag_lag)
        def _():
            wait_mates(1)

        @pl.when((late >= ag_lag) & (late < last))
        def _():
            @pl.loop(*spread(others, late - ag_lag, ag_lag - 1))
            def _(k):
                flip_other(1, k)

            @pl.loop(*spread(units, late - ag_lag, ag_lag - 1))
            def _(u):
                activate(1, u)

    def x_block(owner, b):
        at = pl.ds(pl.multiple_of(owner * dx + b * xcols, 128), xcols)
        return lax.dot_general(
            pg[...], w_all[at, :], (((1,), (1,)), ((), ())),
            preferred_element_type=F32).astype(BF16)

    def x_copy(k):
        return remote(xsend.at[k], xrecv.at[k], x_s.at[k], x_r.at[k],
                      peer(lax.div(k, nb) + 1))

    away = (peers - 1) * nb

    @pl.loop(1, n + 2 * RS_LAG)
    def _(s):
        @pl.when(s == 1)
        def _():
            wait_mates(2)

        for g in range(GROUPS):
            h = s - g * RS_LAG

            @pl.when((h >= 0) & (h < n))
            def _():
                combine(g, h)

            @pl.when((h >= -1) & (h < n - 1))
            def _():
                for d in range(DIRS):
                    make_part(g, d, h + 1)

        @pl.when(s < 3)
        def _():
            @pl.loop(*spread(units, s - 1, 2))
            def _(u):
                activate(2, u)

        e = s - 3

        @pl.when((e >= 0) & (e < 2))
        def _():
            @pl.loop(*spread(away, e, 2))
            def _(k):
                t = lax.div(k, nb) + 1
                xsend[k] = x_block(lax.rem(x + t, peers), lax.rem(k, nb))
                x_copy(k).start()

        @pl.when((e >= 2) & (e < 6))
        def _():
            @pl.loop(*spread(nb, e - 2, 4))
            def _(b):
                xg[:, pl.ds(pl.multiple_of(b * xcols, 128), xcols)] = x_block(x, b)

    @pl.loop(0, nb)
    def _(b):
        at = pl.ds(pl.multiple_of(b * xcols, 128), xcols)
        total = xg[:, at].astype(F32)
        for t in range(1, peers):
            k = (t - 1) * nb + b
            x_copy(k).wait_recv()
            total = total + xrecv[k].astype(F32)
        xg[:, at] = total.astype(BF16)

    @pl.loop(0, n)
    def _(h):
        for g in range(GROUPS):
            for d in range(DIRS):
                rs_mate(g, d, h).wait_send()
                for r in range(SPLIT):
                    ag_mate(g, d, h, r, c).wait_send()

                    @pl.when(h < n - 1)
                    def _():
                        ag_ring(g, d, h, r).wait_send()
                        rs_ring(g, d, h, r).wait_send()

    @pl.loop(0, away)
    def _(k):
        x_copy(k).wait_send()

    for m in range(halves):
        for t in range(1, peers):
            tok_copy(t, m).wait_send()


def on_device(n_dp, peers, tokens, w_in, cotangent):
    n = n_dp // 2
    S, ff = w_in.shape
    rows, dx = tokens.shape
    D = dx * peers
    qcols = ff // (GROUPS * DIRS)
    xcols = min(384, dx)
    nx = (peers - 1) * (dx // xcols)
    slots = GROUPS * DIRS * n
    any_spec = pl.BlockSpec(memory_space=pltpu.HBM)
    vmem = pl.BlockSpec(memory_space=pltpu.VMEM)
    dma = pltpu.SemaphoreType.DMA
    halves = rows // TILE
    return pl.pallas_call(
        functools.partial(kernel, n, peers),
        out_shape=[
            pltpu.VMEM((rows, ff), BF16),
            pltpu.VMEM((rows, dx), BF16),
            pltpu.VMEM((S, ff), BF16),
        ],
        in_specs=[any_spec] * 3,
        out_specs=[vmem] * 3,
        scratch_shapes=[
            pltpu.VMEM((D, ff), BF16),
            pltpu.VMEM((rows, D), BF16),
            pltpu.VMEM((D, rows), BF16),
            pltpu.VMEM((rows, ff), BF16),
            pltpu.VMEM((rows, ff), BF16),
            pltpu.VMEM((GROUPS * DIRS, 2 * S, qcols), F32),
            pltpu.VMEM((slots, S, qcols), BF16),
            pltpu.VMEM((slots, S, qcols), BF16),
            pltpu.VMEM((slots, S, qcols), BF16),
            pltpu.VMEM((slots, S, qcols), BF16),
            pltpu.VMEM((nx, rows, xcols), BF16),
            pltpu.VMEM((nx, rows, xcols), BF16),
            dma((3,)),
            dma(((peers - 1) * halves,)), dma(((peers - 1) * halves,)),
            dma((slots * SPLIT,)), dma((slots * SPLIT,)),
            dma((slots * SPLIT,)), dma((slots * SPLIT,)),
            dma((slots * SPLIT,)), dma((slots * SPLIT,)), dma((slots,)), dma((slots,)),
            dma((nx,)), dma((nx,)),
        ],
        compiler_params=pltpu.CompilerParams(
            collective_id=0, has_side_effects=True,
            vmem_limit_bytes=48 * 1024 * 1024,
        ),
        cost_estimate=pl.CostEstimate(
            flops=6 * rows * D * ff, bytes_accessed=4 * (2 * rows * ff + rows * dx + S * ff),
            transcendentals=rows * ff),
    )(w_in, tokens, cotangent)


def solution(mesh):
    spec = P("dp", "tensor")
    return jax.shard_map(
        functools.partial(on_device, mesh.shape["dp"], mesh.shape["tensor"]),
        mesh=mesh, in_specs=(spec,) * 3, out_specs=(spec,) * 3, check_vma=False,
    )
```

```python
import functools

import jax
import jax.numpy as jnp
from jax import lax
from jax.experimental import pallas as pl
from jax.experimental.pallas import tpu as pltpu
from jax.sharding import PartitionSpec as P

BF16 = jnp.bfloat16
F32 = jnp.float32
GROUPS = 3
DIRS = 2
TILE = 256
SPLIT = 2
AG_LAG = 1
RS_LAG = 2
ROOT = 0.7978845608028654


def kernel(
    n, peers, w_hbm, tok_hbm, cot_hbm, hid, xg, wg,
    w_all, tok, tok_t, cot, pg, part, psend, precv, rsend, rrecv, xsend, xrecv,
    load_sem, tok_s, tok_r, ag_s, ag_r, agp_s, agp_r,
    rs_s, rs_r, rsp_s, rsp_r, x_s, x_r,
):
    S = w_hbm.shape[0]
    rows, dx = tok_hbm.shape
    ff = cot_hbm.shape[1]
    gcols = ff // GROUPS
    qcols = gcols // DIRS
    xcols = xsend.shape[2]
    nb = dx // xcols
    halves = rows // TILE
    ntile = gcols // TILE
    units = halves * ntile
    sr = S // SPLIT

    dp = lax.axis_index("dp")
    x = lax.axis_index("tensor")
    c = lax.rem(dp, 2)
    q = lax.div(dp, 2)
    odd = lax.rem(q, 2)
    p = (1 - odd) * lax.div(q, 2) + odd * (n - lax.div(q + 1, 2))

    def chip_at(pos):
        pos = lax.rem(pos + 2 * n, n)
        far = lax.div(pos, n // 2)
        return (1 - far) * 2 * pos + far * (2 * n - 1 - 2 * pos)

    ring_to = [{"dp": chip_at(p + 1) * 2 + c}, {"dp": chip_at(p - 1) * 2 + c}]
    mate = {"dp": q * 2 + 1 - c}

    def peer(t):
        return {"tensor": lax.rem(x + t, peers)}

    w_loads = [
        pltpu.make_async_copy(
            w_hbm.at[:, pl.ds(k * qcols, qcols)],
            w_all.at[k, pl.ds(pl.multiple_of(dp * S, 16), S)], load_sem.at[2 + k])
        for k in range(GROUPS * DIRS)]
    tok_load = pltpu.make_async_copy(
        tok_hbm, tok.at[:, pl.ds(pl.multiple_of(x * dx, 128), dx)], load_sem.at[0])
    cot_load = pltpu.make_async_copy(cot_hbm, cot, load_sem.at[1])
    for load in w_loads:
        load.start()
    tok_load.start()
    cot_load.start()

    barrier = pltpu.get_barrier_semaphore()
    for who in ring_to + [mate] + [peer(t) for t in range(1, peers)]:
        pl.semaphore_signal(
            barrier, inc=1, device_id=who, device_id_type=pl.DeviceIdType.MESH)
    pl.semaphore_wait(barrier, 3 + peers - 1)

    def remote(src, dst, ssem, rsem, who):
        return pltpu.make_async_remote_copy(
            src_ref=src, dst_ref=dst, send_sem=ssem, recv_sem=rsem,
            device_id=who, device_id_type=pl.DeviceIdType.MESH)

    def w_piece(g, d, pos, core, r):
        owner = chip_at(pos) * 2 + core
        return w_all.at[g * DIRS + d, pl.ds(pl.multiple_of(owner * S + r * sr, 16), sr)]

    def sem_at(g, d, h, r):
        return ((g * DIRS + d) * SPLIT + r) * n + h

    def sign(d):
        return 1 - 2 * d

    def ag_ring(g, d, h, r, back=0):
        piece = w_piece(g, d, p - sign(d) * (h + back), c, r)
        k = sem_at(g, d, h, r)
        return remote(piece, piece, ag_s.at[k], ag_r.at[k], ring_to[d])

    def ag_mate(g, d, h, r, core):
        piece = w_piece(g, d, p - sign(d) * h, core, r)
        k = sem_at(g, d, h, r)
        return remote(piece, piece, agp_s.at[k], agp_r.at[k], mate)

    def tok_copy(t, m):
        piece = tok.at[pl.ds(m * TILE, TILE), pl.ds(pl.multiple_of(x * dx, 128), dx)]
        k = (t - 1) * halves + m
        return remote(piece, piece, tok_s.at[k], tok_r.at[k], peer(t))

    def tok_in(t, m):
        source = lax.rem(x + peers - t, peers)
        piece = tok.at[pl.ds(m * TILE, TILE), pl.ds(pl.multiple_of(source * dx, 128), dx)]
        k = (t - 1) * halves + m
        return remote(piece, piece, tok_s.at[k], tok_r.at[k], peer(t))

    def ag_start(g):
        for r in range(SPLIT):
            for d in range(DIRS):
                ag_ring(g, d, 0, r).start()
        for r in range(SPLIT):
            for d in range(DIRS):
                ag_mate(g, d, 0, r, c).start()

    for load in w_loads:
        load.wait()
    ag_start(0)
    tok_load.wait()
    for m in range(halves):
        for t in range(1, peers):
            tok_copy(t, m).start()
    cot_load.wait()

    def wait_mates(g):
        @pl.loop(0, n)
        def _(h):
            for r in range(SPLIT):
                for d in range(DIRS):
                    ag_mate(g, d, h, r, 1 - c).wait_recv()

    def activate(g, u):
        m = lax.div(u, ntile)
        rsl = pl.ds(pl.multiple_of(m * TILE, TILE), TILE)
        csl = pl.ds(pl.multiple_of(g * gcols + lax.rem(u, ntile) * TILE, TILE), TILE)
        v = jnp.dot(tok[rsl, :], w_all[g * DIRS + lax.rem(u, ntile)],
                    preferred_element_type=F32)
        sq = v * v
        th = jnp.tanh(ROOT * v * (1.0 + 0.044715 * sq))
        half = 0.5 * (1.0 + th)
        hid[rsl, csl] = (v * half).astype(BF16)
        slope = half + 0.5 * v * (1.0 - th * th) * (ROOT * (1.0 + 3.0 * 0.044715 * sq))
        pg[rsl, csl] = (cot[rsl, csl].astype(F32) * slope).astype(BF16)

    def rs_owner(d, h):
        return chip_at(p - sign(d) * (h + 1))

    def slot(g, d, h):
        return (g * DIRS + d) * n + h

    def rs_ring(g, d, h, r):
        k = slot(g, d, h)
        at = pl.ds(r * sr, sr)
        j = sem_at(g, d, h, r)
        return remote(rsend.at[k, at], rrecv.at[k, at], rs_s.at[j], rs_r.at[j], ring_to[d])

    def rs_mate(g, d, h):
        k = slot(g, d, h)
        return remote(psend.at[k], precv.at[k], rsp_s.at[k], rsp_r.at[k], mate)

    def make_part(g, d, h):
        cols = g * gcols + d * qcols
        acc = part.at[g * DIRS + d]
        acc[...] = jnp.dot(
            tok_t[pl.ds(pl.multiple_of(rs_owner(d, h) * 2 * S, 16), 2 * S), :],
            pg[:, cols:cols + qcols], preferred_element_type=F32)
        psend[slot(g, d, h)] = acc[pl.ds(pl.multiple_of((1 - c) * S, 16), S), :].astype(BF16)
        rs_mate(g, d, h).start()

    def combine(g, h):
        for d in range(DIRS):
            rs_mate(g, d, h).wait_recv()
        for r in range(SPLIT):
            for d in range(DIRS):
                combine_piece(g, d, h, r)

    def combine_piece(g, d, h, r):
        k = slot(g, d, h)
        at = pl.ds(r * sr, sr)
        cols = g * gcols + d * qcols
        mine = part[g * DIRS + d, pl.ds(pl.multiple_of(c * S + r * sr, 16), sr), :]
        total = mine + precv[k, at].astype(F32)

        @pl.when(h == 0)
        def _():
            rsend[k, at] = total.astype(BF16)

        @pl.when(h > 0)
        def _():
            rs_ring(g, d, h - 1, r).wait_recv()
            full = (total + rrecv[k - 1, at].astype(F32)).astype(BF16)

            @pl.when(h < n - 1)
            def _():
                rsend[k, at] = full

            @pl.when(h == n - 1)
            def _():
                wg[at, cols:cols + qcols] = full

        @pl.when(h < n - 1)
        def _():
            rs_ring(g, d, h, r).start()

    strips = dx // 128
    others = (peers - 1) * strips

    def spread(count, i, steps):
        return lax.div(i * count, steps), lax.div((i + 1) * count, steps)

    def flip(m, col):
        at = pl.ds(pl.multiple_of(col, 128), 128)
        tok_t[at, m * TILE:(m + 1) * TILE] = tok[m * TILE:(m + 1) * TILE, at].T

    def flip_other(m, k):
        t = lax.div(k, strips) + 1
        flip(m, lax.rem(x + t, peers) * dx + lax.rem(k, strips) * 128)

    def await_tokens(m):
        for t in range(1, peers):
            tok_in(t, m).wait_recv()

    def x_block(owner, b):
        at = pl.ds(pl.multiple_of(owner * dx + b * xcols, 128), xcols)
        rows_of_w = jnp.concatenate(
            [w_all[k, at, :] for k in range(GROUPS * DIRS)], axis=1)
        return lax.dot_general(
            pg[...], rows_of_w, (((1,), (1,)), ((), ())),
            preferred_element_type=F32).astype(BF16)

    def x_copy(k):
        return remote(xsend.at[k], xrecv.at[k], x_s.at[k], x_r.at[k],
                      peer(lax.div(k, nb) + 1))

    away = (peers - 1) * nb

    def ready(g):
        return n - 1 + g * RS_LAG

    done = ready(GROUPS)

    @pl.loop(0, done + n)
    def _(s):
        for g in range(GROUPS):
            h = s - g * AG_LAG

            @pl.when((h >= 0) & (h < n - 1))
            def _():
                for r in range(SPLIT):
                    for d in range(DIRS):
                        ag_ring(g, d, h, r, 1).wait_recv()

                        @pl.when(h < n - 2)
                        def _():
                            ag_ring(g, d, h + 1, r).start()

                        ag_mate(g, d, h + 1, r, c).start()

            if g + 1 < GROUPS:
                @pl.when(h == AG_LAG - 1)
                def _():
                    ag_start(g + 1)

        @pl.when(s < n - 1)
        def _():
            @pl.loop(*spread(strips, s, n - 1))
            def _(k):
                for m in range(halves):
                    flip(m, x * dx + k * 128)

        for g in range(GROUPS):
            i = s - ready(g)
            h = i - RS_LAG

            @pl.when((h >= 0) & (h < n))
            def _():
                combine(g, h)

            @pl.when((i >= 0) & (i < RS_LAG))
            def _():
                @pl.when(i == 0)
                def _():
                    wait_mates(g)

                if g == 0:
                    for m in range(halves):
                        @pl.when(i == m * RS_LAG // halves)
                        def _():
                            await_tokens(m)

                            @pl.loop(0, others)
                            def _(k):
                                flip_other(m, k)

                @pl.loop(*spread(units, i, RS_LAG))
                def _(u):
                    activate(g, u)

            @pl.when((h >= -1) & (h < n - 1))
            def _():
                for d in range(DIRS):
                    make_part(g, d, h + 1)

        e = s - done

        @pl.when((e >= 0) & (e < 2))
        def _():
            @pl.loop(*spread(away, e, 2))
            def _(k):
                t = lax.div(k, nb) + 1
                xsend[k] = x_block(lax.rem(x + t, peers), lax.rem(k, nb))
                x_copy(k).start()

        @pl.when((e >= 2) & (e < 6))
        def _():
            @pl.loop(*spread(nb, e - 2, 4))
            def _(b):
                xg[:, pl.ds(pl.multiple_of(b * xcols, 128), xcols)] = x_block(x, b)

    @pl.loop(0, nb)
    def _(b):
        at = pl.ds(pl.multiple_of(b * xcols, 128), xcols)
        total = xg[:, at].astype(F32)
        for t in range(1, peers):
            k = (t - 1) * nb + b
            x_copy(k).wait_recv()
            total = total + xrecv[k].astype(F32)
        xg[:, at] = total.astype(BF16)

    @pl.loop(0, n)
    def _(h):
        for g in range(GROUPS):
            for d in range(DIRS):
                rs_mate(g, d, h).wait_send()
                for r in range(SPLIT):
                    ag_mate(g, d, h, r, c).wait_send()

                    @pl.when(h < n - 1)
                    def _():
                        ag_ring(g, d, h, r).wait_send()
                        rs_ring(g, d, h, r).wait_send()

    @pl.loop(0, away)
    def _(k):
        x_copy(k).wait_send()

    for m in range(halves):
        for t in range(1, peers):
            tok_copy(t, m).wait_send()


def on_device(n_dp, peers, tokens, w_in, cotangent):
    n = n_dp // 2
    S, ff = w_in.shape
    rows, dx = tokens.shape
    D = dx * peers
    qcols = ff // (GROUPS * DIRS)
    xcols = min(384, dx)
    nx = (peers - 1) * (dx // xcols)
    slots = GROUPS * DIRS * n
    any_spec = pl.BlockSpec(memory_space=pltpu.HBM)
    vmem = pl.BlockSpec(memory_space=pltpu.VMEM)
    dma = pltpu.SemaphoreType.DMA
    halves = rows // TILE
    return pl.pallas_call(
        functools.partial(kernel, n, peers),
        out_shape=[
            pltpu.VMEM((rows, ff), BF16),
            pltpu.VMEM((rows, dx), BF16),
            pltpu.VMEM((S, ff), BF16),
        ],
        in_specs=[any_spec] * 3,
        out_specs=[vmem] * 3,
        scratch_shapes=[
            pltpu.VMEM((GROUPS * DIRS, D, qcols), BF16),
            pltpu.VMEM((rows, D), BF16),
            pltpu.VMEM((D, rows), BF16),
            pltpu.VMEM((rows, ff), BF16),
            pltpu.VMEM((rows, ff), BF16),
            pltpu.VMEM((GROUPS * DIRS, 2 * S, qcols), F32),
            pltpu.VMEM((slots, S, qcols), BF16),
            pltpu.VMEM((slots, S, qcols), BF16),
            pltpu.VMEM((slots, S, qcols), BF16),
            pltpu.VMEM((slots, S, qcols), BF16),
            pltpu.VMEM((nx, rows, xcols), BF16),
            pltpu.VMEM((nx, rows, xcols), BF16),
            dma((2 + GROUPS * DIRS,)),
            dma(((peers - 1) * halves,)), dma(((peers - 1) * halves,)),
            dma((slots * SPLIT,)), dma((slots * SPLIT,)),
            dma((slots * SPLIT,)), dma((slots * SPLIT,)),
            dma((slots * SPLIT,)), dma((slots * SPLIT,)), dma((slots,)), dma((slots,)),
            dma((nx,)), dma((nx,)),
        ],
        compiler_params=pltpu.CompilerParams(
            collective_id=0, has_side_effects=True,
            vmem_limit_bytes=60 * 1024 * 1024,
        ),
        cost_estimate=pl.CostEstimate(
            flops=6 * rows * D * ff, bytes_accessed=4 * (2 * rows * ff + rows * dx + S * ff),
            transcendentals=rows * ff),
    )(w_in, tokens, cotangent)


def solution(mesh):
    spec = P("dp", "tensor")
    return jax.shard_map(
        functools.partial(on_device, mesh.shape["dp"], mesh.shape["tensor"]),
        mesh=mesh, in_specs=(spec,) * 3, out_specs=(spec,) * 3, check_vma=False,
    )
```

```python
import functools

import jax
import jax.numpy as jnp
from jax import lax
from jax.experimental import pallas as pl
from jax.experimental.pallas import tpu as pltpu
from jax.sharding import PartitionSpec as P

BF16 = jnp.bfloat16
F32 = jnp.float32
GROUPS = 3
DIRS = 2
TILE = 256
SPLIT = 2
AG_LAG = 2
READY = (-1, 1, 3)
REDUCE = (1, 3, 4)
ROOT = 0.7978845608028654


def kernel(
    n, peers, w_hbm, tok_hbm, cot_hbm, hid, xg, wg,
    w_all, tok, tok_t, cot, pg, part, psend, precv, rsend, rrecv, xsend, xrecv,
    load_sem, tok_s, tok_r, ag_s, ag_r, agp_s, agp_r,
    rs_s, rs_r, rsp_s, rsp_r, x_s, x_r,
):
    S = w_hbm.shape[0]
    rows, dx = tok_hbm.shape
    ff = cot_hbm.shape[1]
    gcols = ff // GROUPS
    qcols = gcols // DIRS
    xcols = xsend.shape[2]
    nb = dx // xcols
    halves = rows // TILE
    ntile = gcols // TILE
    units = halves * ntile
    sr = S // SPLIT

    dp = lax.axis_index("dp")
    x = lax.axis_index("tensor")
    c = lax.rem(dp, 2)
    q = lax.div(dp, 2)
    odd = lax.rem(q, 2)
    p = (1 - odd) * lax.div(q, 2) + odd * (n - lax.div(q + 1, 2))

    def chip_at(pos):
        pos = lax.rem(pos + 2 * n, n)
        far = lax.div(pos, n // 2)
        return (1 - far) * 2 * pos + far * (2 * n - 1 - 2 * pos)

    ring_to = [{"dp": chip_at(p + 1) * 2 + c}, {"dp": chip_at(p - 1) * 2 + c}]
    mate = {"dp": q * 2 + 1 - c}

    def peer(t):
        return {"tensor": lax.rem(x + t, peers)}

    w_loads = [
        pltpu.make_async_copy(
            w_hbm.at[:, pl.ds(k * qcols, qcols)],
            w_all.at[k, pl.ds(pl.multiple_of(dp * S, 16), S)], load_sem.at[2 + k])
        for k in range(GROUPS * DIRS)]
    tok_load = pltpu.make_async_copy(
        tok_hbm, tok.at[:, pl.ds(pl.multiple_of(x * dx, 128), dx)], load_sem.at[0])
    cot_load = pltpu.make_async_copy(cot_hbm, cot, load_sem.at[1])
    for load in w_loads:
        load.start()
    tok_load.start()
    cot_load.start()

    barrier = pltpu.get_barrier_semaphore()
    for who in ring_to + [mate] + [peer(t) for t in range(1, peers)]:
        pl.semaphore_signal(
            barrier, inc=1, device_id=who, device_id_type=pl.DeviceIdType.MESH)
    pl.semaphore_wait(barrier, 3 + peers - 1)

    def remote(src, dst, ssem, rsem, who):
        return pltpu.make_async_remote_copy(
            src_ref=src, dst_ref=dst, send_sem=ssem, recv_sem=rsem,
            device_id=who, device_id_type=pl.DeviceIdType.MESH)

    def w_piece(g, d, pos, core, r):
        owner = chip_at(pos) * 2 + core
        return w_all.at[g * DIRS + d, pl.ds(pl.multiple_of(owner * S + r * sr, 16), sr)]

    def sem_at(g, d, h, r):
        return ((g * DIRS + d) * SPLIT + r) * n + h

    def sign(d):
        return 1 - 2 * d

    def ag_ring(g, d, h, r, back=0):
        piece = w_piece(g, d, p - sign(d) * (h + back), c, r)
        k = sem_at(g, d, h, r)
        return remote(piece, piece, ag_s.at[k], ag_r.at[k], ring_to[d])

    def ag_mate(g, d, h, r, core):
        piece = w_piece(g, d, p - sign(d) * h, core, r)
        k = sem_at(g, d, h, r)
        return remote(piece, piece, agp_s.at[k], agp_r.at[k], mate)

    def tok_copy(t, m):
        piece = tok.at[pl.ds(m * TILE, TILE), pl.ds(pl.multiple_of(x * dx, 128), dx)]
        k = (t - 1) * halves + m
        return remote(piece, piece, tok_s.at[k], tok_r.at[k], peer(t))

    def tok_in(t, m):
        source = lax.rem(x + peers - t, peers)
        piece = tok.at[pl.ds(m * TILE, TILE), pl.ds(pl.multiple_of(source * dx, 128), dx)]
        k = (t - 1) * halves + m
        return remote(piece, piece, tok_s.at[k], tok_r.at[k], peer(t))

    def ag_start(g):
        for r in range(SPLIT):
            for d in range(DIRS):
                ag_ring(g, d, 0, r).start()
        for r in range(SPLIT):
            for d in range(DIRS):
                ag_mate(g, d, 0, r, c).start()

    for load in w_loads:
        load.wait()
    ag_start(0)
    tok_load.wait()
    for m in range(halves):
        for t in range(1, peers):
            tok_copy(t, m).start()
    cot_load.wait()

    def wait_mates(g):
        @pl.loop(0, n)
        def _(h):
            for r in range(SPLIT):
                for d in range(DIRS):
                    ag_mate(g, d, h, r, 1 - c).wait_recv()

    def activate(g, u):
        m = lax.div(u, ntile)
        rsl = pl.ds(pl.multiple_of(m * TILE, TILE), TILE)
        csl = pl.ds(pl.multiple_of(g * gcols + lax.rem(u, ntile) * TILE, TILE), TILE)
        v = jnp.dot(tok[rsl, :], w_all[g * DIRS + lax.rem(u, ntile)],
                    preferred_element_type=F32)
        sq = v * v
        th = jnp.tanh(ROOT * v * (1.0 + 0.044715 * sq))
        half = 0.5 * (1.0 + th)
        hid[rsl, csl] = (v * half).astype(BF16)
        slope = half + 0.5 * v * (1.0 - th * th) * (ROOT * (1.0 + 3.0 * 0.044715 * sq))
        pg[rsl, csl] = (cot[rsl, csl].astype(F32) * slope).astype(BF16)

    def rs_owner(d, h):
        return chip_at(p - sign(d) * (h + 1))

    def slot(g, d, h):
        return (g * DIRS + d) * n + h

    def rs_ring(g, d, h, r):
        k = slot(g, d, h)
        at = pl.ds(r * sr, sr)
        j = sem_at(g, d, h, r)
        return remote(rsend.at[k, at], rrecv.at[k, at], rs_s.at[j], rs_r.at[j], ring_to[d])

    def rs_mate(g, d, h):
        k = slot(g, d, h)
        return remote(psend.at[k], precv.at[k], rsp_s.at[k], rsp_r.at[k], mate)

    def make_part(g, d, h):
        cols = g * gcols + d * qcols
        acc = part.at[g * DIRS + d]
        acc[...] = jnp.dot(
            tok_t[pl.ds(pl.multiple_of(rs_owner(d, h) * 2 * S, 16), 2 * S), :],
            pg[:, cols:cols + qcols], preferred_element_type=F32)
        psend[slot(g, d, h)] = acc[pl.ds(pl.multiple_of((1 - c) * S, 16), S), :].astype(BF16)
        rs_mate(g, d, h).start()

    def combine(g, h):
        for d in range(DIRS):
            rs_mate(g, d, h).wait_recv()
        for r in range(SPLIT):
            for d in range(DIRS):
                combine_piece(g, d, h, r)

    def combine_piece(g, d, h, r):
        k = slot(g, d, h)
        at = pl.ds(r * sr, sr)
        cols = g * gcols + d * qcols
        mine = part[g * DIRS + d, pl.ds(pl.multiple_of(c * S + r * sr, 16), sr), :]
        total = mine + precv[k, at].astype(F32)

        @pl.when(h == 0)
        def _():
            rsend[k, at] = total.astype(BF16)

        @pl.when(h > 0)
        def _():
            rs_ring(g, d, h - 1, r).wait_recv()
            full = (total + rrecv[k - 1, at].astype(F32)).astype(BF16)

            @pl.when(h < n - 1)
            def _():
                rsend[k, at] = full

            @pl.when(h == n - 1)
            def _():
                wg[at, cols:cols + qcols] = full

        @pl.when(h < n - 1)
        def _():
            rs_ring(g, d, h, r).start()

    strips = dx // 128
    others = (peers - 1) * strips

    def spread(count, i, steps):
        return lax.div(i * count, steps), lax.div((i + 1) * count, steps)

    def flip(m, col):
        at = pl.ds(pl.multiple_of(col, 128), 128)
        tok_t[at, m * TILE:(m + 1) * TILE] = tok[m * TILE:(m + 1) * TILE, at].T

    def flip_other(m, k):
        t = lax.div(k, strips) + 1
        flip(m, lax.rem(x + t, peers) * dx + lax.rem(k, strips) * 128)

    def await_tokens(m):
        for t in range(1, peers):
            tok_in(t, m).wait_recv()

    def x_block(owner, b):
        at = pl.ds(pl.multiple_of(owner * dx + b * xcols, 128), xcols)
        rows_of_w = jnp.concatenate(
            [w_all[k, at, :] for k in range(GROUPS * DIRS)], axis=1)
        return lax.dot_general(
            pg[...], rows_of_w, (((1,), (1,)), ((), ())),
            preferred_element_type=F32).astype(BF16)

    def x_copy(k):
        return remote(xsend.at[k], xrecv.at[k], x_s.at[k], x_r.at[k],
                      peer(lax.div(k, nb) + 1))

    away = (peers - 1) * nb

    done = n + REDUCE[-1]

    @pl.loop(0, done + n)
    def _(s):
        for g in range(GROUPS):
            h = s - g * AG_LAG

            @pl.when((h >= 0) & (h < n - 1))
            def _():
                for r in range(SPLIT):
                    for d in range(DIRS):
                        ag_ring(g, d, h, r, 1).wait_recv()

                        @pl.when(h < n - 2)
                        def _():
                            ag_ring(g, d, h + 1, r).start()

                        ag_mate(g, d, h + 1, r, c).start()

            if g + 1 < GROUPS:
                @pl.when(h == AG_LAG - 1)
                def _():
                    ag_start(g + 1)

        @pl.when(s < n - 1)
        def _():
            @pl.loop(*spread(strips, s, n - 1))
            def _(k):
                for m in range(halves):
                    flip(m, x * dx + k * 128)

        for g in range(GROUPS):
            i = s - n - READY[g]
            h = s - n - REDUCE[g]
            span = REDUCE[g] - READY[g]

            @pl.when((h >= 0) & (h < n))
            def _():
                combine(g, h)

            @pl.when((i >= 0) & (i < span))
            def _():
                @pl.when(i == 0)
                def _():
                    wait_mates(g)

                if g == 0:
                    for m in range(halves):
                        @pl.when(i == m * span // halves)
                        def _():
                            await_tokens(m)

                            @pl.loop(0, others)
                            def _(k):
                                flip_other(m, k)

                @pl.loop(*spread(units, i, span))
                def _(u):
                    activate(g, u)

            @pl.when((h >= -1) & (h < n - 1))
            def _():
                for d in range(DIRS):
                    make_part(g, d, h + 1)

        e = s - done

        @pl.when(e == 0)
        def _():
            @pl.loop(0, away)
            def _(k):
                t = lax.div(k, nb) + 1
                xsend[k] = x_block(lax.rem(x + t, peers), lax.rem(k, nb))
                x_copy(k).start()

        @pl.when((e >= 2) & (e < 6))
        def _():
            @pl.loop(*spread(nb, e - 2, 4))
            def _(b):
                xg[:, pl.ds(pl.multiple_of(b * xcols, 128), xcols)] = x_block(x, b)

    @pl.loop(0, nb)
    def _(b):
        at = pl.ds(pl.multiple_of(b * xcols, 128), xcols)
        total = xg[:, at].astype(F32)
        for t in range(1, peers):
            k = (t - 1) * nb + b
            x_copy(k).wait_recv()
            total = total + xrecv[k].astype(F32)
        xg[:, at] = total.astype(BF16)

    @pl.loop(0, n)
    def _(h):
        for g in range(GROUPS):
            for d in range(DIRS):
                rs_mate(g, d, h).wait_send()
                for r in range(SPLIT):
                    ag_mate(g, d, h, r, c).wait_send()

                    @pl.when(h < n - 1)
                    def _():
                        ag_ring(g, d, h, r).wait_send()
                        rs_ring(g, d, h, r).wait_send()

    @pl.loop(0, away)
    def _(k):
        x_copy(k).wait_send()

    for m in range(halves):
        for t in range(1, peers):
            tok_copy(t, m).wait_send()


def on_device(n_dp, peers, tokens, w_in, cotangent):
    n = n_dp // 2
    S, ff = w_in.shape
    rows, dx = tokens.shape
    D = dx * peers
    qcols = ff // (GROUPS * DIRS)
    xcols = min(384, dx)
    nx = (peers - 1) * (dx // xcols)
    slots = GROUPS * DIRS * n
    any_spec = pl.BlockSpec(memory_space=pltpu.HBM)
    vmem = pl.BlockSpec(memory_space=pltpu.VMEM)
    dma = pltpu.SemaphoreType.DMA
    halves = rows // TILE
    return pl.pallas_call(
        functools.partial(kernel, n, peers),
        out_shape=[
            pltpu.VMEM((rows, ff), BF16),
            pltpu.VMEM((rows, dx), BF16),
            pltpu.VMEM((S, ff), BF16),
        ],
        in_specs=[any_spec] * 3,
        out_specs=[vmem] * 3,
        scratch_shapes=[
            pltpu.VMEM((GROUPS * DIRS, D, qcols), BF16),
            pltpu.VMEM((rows, D), BF16),
            pltpu.VMEM((D, rows), BF16),
            pltpu.VMEM((rows, ff), BF16),
            pltpu.VMEM((rows, ff), BF16),
            pltpu.VMEM((GROUPS * DIRS, 2 * S, qcols), F32),
            pltpu.VMEM((slots, S, qcols), BF16),
            pltpu.VMEM((slots, S, qcols), BF16),
            pltpu.VMEM((slots, S, qcols), BF16),
            pltpu.VMEM((slots, S, qcols), BF16),
            pltpu.VMEM((nx, rows, xcols), BF16),
            pltpu.VMEM((nx, rows, xcols), BF16),
            dma((2 + GROUPS * DIRS,)),
            dma(((peers - 1) * halves,)), dma(((peers - 1) * halves,)),
            dma((slots * SPLIT,)), dma((slots * SPLIT,)),
            dma((slots * SPLIT,)), dma((slots * SPLIT,)),
            dma((slots * SPLIT,)), dma((slots * SPLIT,)), dma((slots,)), dma((slots,)),
            dma((nx,)), dma((nx,)),
        ],
        compiler_params=pltpu.CompilerParams(
            collective_id=0, has_side_effects=True,
            vmem_limit_bytes=60 * 1024 * 1024,
        ),
        cost_estimate=pl.CostEstimate(
            flops=6 * rows * D * ff, bytes_accessed=4 * (2 * rows * ff + rows * dx + S * ff),
            transcendentals=rows * ff),
    )(w_in, tokens, cotangent)


def solution(mesh):
    spec = P("dp", "tensor")
    return jax.shard_map(
        functools.partial(on_device, mesh.shape["dp"], mesh.shape["tensor"]),
        mesh=mesh, in_specs=(spec,) * 3, out_specs=(spec,) * 3, check_vma=False,
    )
```

```python
import functools

import jax
import jax.numpy as jnp
from jax import lax
from jax.experimental import pallas as pl
from jax.experimental.pallas import tpu as pltpu
from jax.sharding import PartitionSpec as P

BF16 = jnp.bfloat16
F32 = jnp.float32
GROUPS = 3
DIRS = 2
TILE = 256
SPLIT = 2
AG_LAG = 2
READY = (-1, 1, 3)
REDUCE = (1, 3, 4)
ROOT = 0.7978845608028654


def kernel(
    n, peers, w_hbm, tok_hbm, cot_hbm, hid, xg, wg,
    w_all, tok, tok_t, cot, pg, part, psend, precv, rsend, rrecv, xsend, xrecv,
    load_sem, tok_s, tok_r, ag_s, ag_r, agp_s, agp_r,
    rs_s, rs_r, rsp_s, rsp_r, x_s, x_r,
):
    S = w_hbm.shape[0]
    rows, dx = tok_hbm.shape
    ff = cot_hbm.shape[1]
    gcols = ff // GROUPS
    qcols = gcols // DIRS
    xcols = xsend.shape[2]
    nb = dx // xcols
    halves = rows // TILE
    ntile = gcols // TILE
    units = halves * ntile
    sr = S // SPLIT

    dp = lax.axis_index("dp")
    x = lax.axis_index("tensor")
    c = lax.rem(dp, 2)
    q = lax.div(dp, 2)
    odd = lax.rem(q, 2)
    p = (1 - odd) * lax.div(q, 2) + odd * (n - lax.div(q + 1, 2))

    def chip_at(pos):
        pos = lax.rem(pos + 2 * n, n)
        far = lax.div(pos, n // 2)
        return (1 - far) * 2 * pos + far * (2 * n - 1 - 2 * pos)

    ring_to = [{"dp": chip_at(p + 1) * 2 + c}, {"dp": chip_at(p - 1) * 2 + c}]
    mate = {"dp": q * 2 + 1 - c}

    def peer(t):
        return {"tensor": lax.rem(x + t, peers)}

    w_loads = [
        pltpu.make_async_copy(
            w_hbm.at[:, pl.ds(k * qcols, qcols)],
            w_all.at[k, pl.ds(pl.multiple_of(dp * S, 16), S)], load_sem.at[2 + k])
        for k in range(GROUPS * DIRS)]
    tok_load = pltpu.make_async_copy(
        tok_hbm, tok.at[:, pl.ds(pl.multiple_of(x * dx, 128), dx)], load_sem.at[0])
    cot_load = pltpu.make_async_copy(cot_hbm, cot, load_sem.at[1])
    for load in w_loads:
        load.start()
    tok_load.start()
    cot_load.start()

    barrier = pltpu.get_barrier_semaphore()
    for who in ring_to + [mate] + [peer(t) for t in range(1, peers)]:
        pl.semaphore_signal(
            barrier, inc=1, device_id=who, device_id_type=pl.DeviceIdType.MESH)
    pl.semaphore_wait(barrier, 3 + peers - 1)

    def remote(src, dst, ssem, rsem, who):
        return pltpu.make_async_remote_copy(
            src_ref=src, dst_ref=dst, send_sem=ssem, recv_sem=rsem,
            device_id=who, device_id_type=pl.DeviceIdType.MESH)

    def w_piece(g, d, pos, core, r):
        owner = chip_at(pos) * 2 + core
        return w_all.at[g * DIRS + d, pl.ds(pl.multiple_of(owner * S + r * sr, 16), sr)]

    def sem_at(g, d, h, r):
        return ((g * DIRS + d) * SPLIT + r) * n + h

    def sign(d):
        return 1 - 2 * d

    def ag_ring(g, d, h, r, back=0):
        piece = w_piece(g, d, p - sign(d) * (h + back), c, r)
        k = sem_at(g, d, h, r)
        return remote(piece, piece, ag_s.at[k], ag_r.at[k], ring_to[d])

    def ag_mate(g, d, h, r, core):
        piece = w_piece(g, d, p - sign(d) * h, core, r)
        k = sem_at(g, d, h, r)
        return remote(piece, piece, agp_s.at[k], agp_r.at[k], mate)

    def tok_copy(t, m):
        piece = tok.at[pl.ds(m * TILE, TILE), pl.ds(pl.multiple_of(x * dx, 128), dx)]
        k = (t - 1) * halves + m
        return remote(piece, piece, tok_s.at[k], tok_r.at[k], peer(t))

    def tok_in(t, m):
        source = lax.rem(x + peers - t, peers)
        piece = tok.at[pl.ds(m * TILE, TILE), pl.ds(pl.multiple_of(source * dx, 128), dx)]
        k = (t - 1) * halves + m
        return remote(piece, piece, tok_s.at[k], tok_r.at[k], peer(t))

    def ag_start(g):
        for r in range(SPLIT):
            for d in range(DIRS):
                ag_ring(g, d, 0, r).start()
        for r in range(SPLIT):
            for d in range(DIRS):
                ag_mate(g, d, 0, r, c).start()

    for load in w_loads:
        load.wait()
    ag_start(0)
    tok_load.wait()
    for m in range(halves):
        for t in range(1, peers):
            tok_copy(t, m).start()
    cot_load.wait()

    def wait_mates(g):
        @pl.loop(0, n)
        def _(h):
            for r in range(SPLIT):
                for d in range(DIRS):
                    ag_mate(g, d, h, r, 1 - c).wait_recv()

    def activate(g, u):
        m = lax.div(u, ntile)
        rsl = pl.ds(pl.multiple_of(m * TILE, TILE), TILE)
        csl = pl.ds(pl.multiple_of(g * gcols + lax.rem(u, ntile) * TILE, TILE), TILE)
        v = jnp.dot(tok[rsl, :], w_all[g * DIRS + lax.rem(u, ntile)],
                    preferred_element_type=F32)
        sq = v * v
        th = jnp.tanh(ROOT * v * (1.0 + 0.044715 * sq))
        half = 0.5 * (1.0 + th)
        hid[rsl, csl] = (v * half).astype(BF16)
        slope = half + 0.5 * v * (1.0 - th * th) * (ROOT * (1.0 + 3.0 * 0.044715 * sq))
        pg[rsl, csl] = (cot[rsl, csl].astype(F32) * slope).astype(BF16)

    def rs_owner(d, h):
        return chip_at(p - sign(d) * (h + 1))

    def slot(g, d, h):
        return (g * DIRS + d) * n + h

    def rs_ring(g, d, h, r):
        k = slot(g, d, h)
        at = pl.ds(r * sr, sr)
        j = sem_at(g, d, h, r)
        return remote(rsend.at[k, at], rrecv.at[k, at], rs_s.at[j], rs_r.at[j], ring_to[d])

    def rs_mate(g, d, h):
        k = slot(g, d, h)
        return remote(psend.at[k], precv.at[k], rsp_s.at[k], rsp_r.at[k], mate)

    def make_part(g, d, h):
        cols = g * gcols + d * qcols
        acc = part.at[g * DIRS + d]
        acc[...] = jnp.dot(
            tok_t[pl.ds(pl.multiple_of(rs_owner(d, h) * 2 * S, 16), 2 * S), :],
            pg[:, cols:cols + qcols], preferred_element_type=F32)
        psend[slot(g, d, h)] = acc[pl.ds(pl.multiple_of((1 - c) * S, 16), S), :].astype(BF16)
        rs_mate(g, d, h).start()

    def combine(g, h):
        for d in range(DIRS):
            rs_mate(g, d, h).wait_recv()
        for r in range(SPLIT):
            for d in range(DIRS):
                combine_piece(g, d, h, r)

    def combine_piece(g, d, h, r):
        k = slot(g, d, h)
        at = pl.ds(r * sr, sr)
        cols = g * gcols + d * qcols
        mine = part[g * DIRS + d, pl.ds(pl.multiple_of(c * S + r * sr, 16), sr), :]
        total = mine + precv[k, at].astype(F32)

        @pl.when(h == 0)
        def _():
            rsend[k, at] = total.astype(BF16)

        @pl.when(h > 0)
        def _():
            rs_ring(g, d, h - 1, r).wait_recv()
            full = (total + rrecv[k - 1, at].astype(F32)).astype(BF16)

            @pl.when(h < n - 1)
            def _():
                rsend[k, at] = full

            @pl.when(h == n - 1)
            def _():
                wg[at, cols:cols + qcols] = full

        @pl.when(h < n - 1)
        def _():
            rs_ring(g, d, h, r).start()

    strips = dx // 128
    others = (peers - 1) * strips

    def spread(count, i, steps):
        return lax.div(i * count, steps), lax.div((i + 1) * count, steps)

    def flip(m, col):
        at = pl.ds(pl.multiple_of(col, 128), 128)
        tok_t[at, m * TILE:(m + 1) * TILE] = tok[m * TILE:(m + 1) * TILE, at].T

    def flip_other(m, k):
        t = lax.div(k, strips) + 1
        flip(m, lax.rem(x + t, peers) * dx + lax.rem(k, strips) * 128)

    def await_tokens(m):
        for t in range(1, peers):
            tok_in(t, m).wait_recv()

    def x_block(owner, b):
        at = pl.ds(pl.multiple_of(owner * dx + b * xcols, 128), xcols)
        rows_of_w = jnp.concatenate(
            [w_all[k, at, :] for k in range(GROUPS * DIRS)], axis=1)
        return lax.dot_general(
            pg[...], rows_of_w, (((1,), (1,)), ((), ())),
            preferred_element_type=F32).astype(BF16)

    def x_copy(k):
        return remote(xsend.at[k], xrecv.at[k], x_s.at[k], x_r.at[k],
                      peer(lax.div(k, nb) + 1))

    away = (peers - 1) * nb

    done = n + REDUCE[-1]

    @pl.loop(0, done + n)
    def _(s):
        for g in range(GROUPS):
            h = s - g * AG_LAG

            @pl.when((h >= 0) & (h < n - 1))
            def _():
                for r in range(SPLIT):
                    for d in range(DIRS):
                        ag_ring(g, d, h, r, 1).wait_recv()

                        @pl.when(h < n - 2)
                        def _():
                            ag_ring(g, d, h + 1, r).start()

                        ag_mate(g, d, h + 1, r, c).start()

            if g + 1 < GROUPS:
                @pl.when(h == AG_LAG - 1)
                def _():
                    ag_start(g + 1)

        @pl.when(s < n - 1)
        def _():
            @pl.loop(*spread(strips, s, n - 1))
            def _(k):
                for m in range(halves):
                    flip(m, x * dx + k * 128)

        for g in range(GROUPS):
            i = s - n - READY[g]
            h = s - n - REDUCE[g]
            span = REDUCE[g] - READY[g]

            @pl.when((h >= 0) & (h < n))
            def _():
                combine(g, h)

            @pl.when((i >= 0) & (i < span))
            def _():
                @pl.when(i == 0)
                def _():
                    wait_mates(g)

                if g == 0:
                    for m in range(halves):
                        @pl.when(i == m * span // halves)
                        def _():
                            await_tokens(m)

                            @pl.loop(0, others)
                            def _(k):
                                flip_other(m, k)

                @pl.loop(*spread(units, i, span))
                def _(u):
                    activate(g, u)

            @pl.when((h >= -1) & (h < n - 1))
            def _():
                for d in range(DIRS):
                    make_part(g, d, h + 1)

        e = s - done

        @pl.when(e == 0)
        def _():
            @pl.loop(0, away)
            def _(k):
                t = lax.div(k, nb) + 1
                xsend[k] = x_block(lax.rem(x + t, peers), lax.rem(k, nb))
                x_copy(k).start()

        @pl.when((e >= 2) & (e < 6))
        def _():
            @pl.loop(*spread(nb, e - 2, 4))
            def _(b):
                xg[:, pl.ds(pl.multiple_of(b * xcols, 128), xcols)] = x_block(x, b)

        @pl.when((e >= 0) & (e < n))
        def _():
            for g in range(GROUPS):
                for d in range(DIRS):
                    for r in range(SPLIT):
                        ag_mate(g, d, e, r, c).wait_send()

                        @pl.when(e < n - 1)
                        def _():
                            ag_ring(g, d, e, r).wait_send()

        for g in range(GROUPS):
            h = s - n - REDUCE[g]

            @pl.when((h >= 2) & (h < n))
            def _():
                for d in range(DIRS):
                    rs_mate(g, d, h - 2).wait_send()
                    for r in range(SPLIT):
                        rs_ring(g, d, h - 2, r).wait_send()

    @pl.loop(0, nb)
    def _(b):
        at = pl.ds(pl.multiple_of(b * xcols, 128), xcols)
        total = xg[:, at].astype(F32)
        for t in range(1, peers):
            k = (t - 1) * nb + b
            x_copy(k).wait_recv()
            total = total + xrecv[k].astype(F32)
        xg[:, at] = total.astype(BF16)

    for g in range(GROUPS):
        for d in range(DIRS):
            for h in (n - 2, n - 1):
                rs_mate(g, d, h).wait_send()
            for r in range(SPLIT):
                rs_ring(g, d, n - 2, r).wait_send()

    @pl.loop(0, away)
    def _(k):
        x_copy(k).wait_send()

    for m in range(halves):
        for t in range(1, peers):
            tok_copy(t, m).wait_send()


def store(*refs):
    sems = refs[6]
    copies = [
        pltpu.make_async_copy(refs[k], refs[3 + k], sems.at[k]) for k in range(3)]
    for copy in copies:
        copy.start()
    for copy in copies:
        copy.wait()


def on_device(n_dp, peers, tokens, w_in, cotangent):
    n = n_dp // 2
    S, ff = w_in.shape
    rows, dx = tokens.shape
    D = dx * peers
    qcols = ff // (GROUPS * DIRS)
    xcols = min(384, dx)
    nx = (peers - 1) * (dx // xcols)
    slots = GROUPS * DIRS * n
    any_spec = pl.BlockSpec(memory_space=pltpu.HBM)
    vmem = pl.BlockSpec(memory_space=pltpu.VMEM)
    dma = pltpu.SemaphoreType.DMA
    halves = rows // TILE
    results = pl.pallas_call(
        functools.partial(kernel, n, peers),
        out_shape=[
            pltpu.VMEM((rows, ff), BF16),
            pltpu.VMEM((rows, dx), BF16),
            pltpu.VMEM((S, ff), BF16),
        ],
        in_specs=[any_spec] * 3,
        out_specs=[vmem] * 3,
        scratch_shapes=[
            pltpu.VMEM((GROUPS * DIRS, D, qcols), BF16),
            pltpu.VMEM((rows, D), BF16),
            pltpu.VMEM((D, rows), BF16),
            pltpu.VMEM((rows, ff), BF16),
            pltpu.VMEM((rows, ff), BF16),
            pltpu.VMEM((GROUPS * DIRS, 2 * S, qcols), F32),
            pltpu.VMEM((slots, S, qcols), BF16),
            pltpu.VMEM((slots, S, qcols), BF16),
            pltpu.VMEM((slots, S, qcols), BF16),
            pltpu.VMEM((slots, S, qcols), BF16),
            pltpu.VMEM((nx, rows, xcols), BF16),
            pltpu.VMEM((nx, rows, xcols), BF16),
            dma((2 + GROUPS * DIRS,)),
            dma(((peers - 1) * halves,)), dma(((peers - 1) * halves,)),
            dma((slots * SPLIT,)), dma((slots * SPLIT,)),
            dma((slots * SPLIT,)), dma((slots * SPLIT,)),
            dma((slots * SPLIT,)), dma((slots * SPLIT,)), dma((slots,)), dma((slots,)),
            dma((nx,)), dma((nx,)),
        ],
        compiler_params=pltpu.CompilerParams(
            collective_id=0, has_side_effects=True,
            vmem_limit_bytes=60 * 1024 * 1024,
        ),
        cost_estimate=pl.CostEstimate(
            flops=6 * rows * D * ff, bytes_accessed=4 * (2 * rows * ff + rows * dx + S * ff),
            transcendentals=rows * ff),
    )(w_in, tokens, cotangent)
    return pl.pallas_call(
        store,
        out_shape=[
            jax.ShapeDtypeStruct((rows, ff), BF16),
            jax.ShapeDtypeStruct((rows, dx), BF16),
            jax.ShapeDtypeStruct((S, ff), BF16),
        ],
        in_specs=[vmem] * 3,
        out_specs=[any_spec] * 3,
        scratch_shapes=[dma((3,))],
    )(*results)


def solution(mesh):
    spec = P("dp", "tensor")
    return jax.shard_map(
        functools.partial(on_device, mesh.shape["dp"], mesh.shape["tensor"]),
        mesh=mesh, in_specs=(spec,) * 3, out_specs=(spec,) * 3, check_vma=False,
    )
```

```python
import functools

import jax
import jax.numpy as jnp
from jax import lax
from jax.experimental import pallas as pl
from jax.experimental.pallas import tpu as pltpu
from jax.sharding import PartitionSpec as P

BF16 = jnp.bfloat16
F32 = jnp.float32
GROUPS = 3
DIRS = 2
TILE = 256
SPLIT = 1
AG_LAG = 2
READY = (-1, 1, 3)
REDUCE = (1, 3, 4)
ROOT = 0.7978845608028654


def kernel(
    n, peers, w_hbm, tok_hbm, cot_hbm, hid, xg, wg,
    w_all, tok, tok_t, cot, pg, part, psend, precv, rsend, rrecv, xsend, xrecv,
    load_sem, tok_s, tok_r, ag_s, ag_r, agp_s, agp_r,
    rs_s, rs_r, rsp_s, rsp_r, x_s, x_r,
):
    S = w_hbm.shape[0]
    rows, dx = tok_hbm.shape
    ff = cot_hbm.shape[1]
    gcols = ff // GROUPS
    qcols = gcols // DIRS
    xcols = xsend.shape[2]
    nb = dx // xcols
    halves = rows // TILE
    ntile = gcols // TILE
    units = halves * ntile
    sr = S // SPLIT

    dp = lax.axis_index("dp")
    x = lax.axis_index("tensor")
    c = lax.rem(dp, 2)
    q = lax.div(dp, 2)
    odd = lax.rem(q, 2)
    p = (1 - odd) * lax.div(q, 2) + odd * (n - lax.div(q + 1, 2))

    def chip_at(pos):
        pos = lax.rem(pos + 2 * n, n)
        far = lax.div(pos, n // 2)
        return (1 - far) * 2 * pos + far * (2 * n - 1 - 2 * pos)

    ring_to = [{"dp": chip_at(p + 1) * 2 + c}, {"dp": chip_at(p - 1) * 2 + c}]
    mate = {"dp": q * 2 + 1 - c}

    def peer(t):
        return {"tensor": lax.rem(x + t, peers)}

    w_loads = [
        pltpu.make_async_copy(
            w_hbm.at[:, pl.ds(k * qcols, qcols)],
            w_all.at[k, pl.ds(pl.multiple_of(dp * S, 16), S)], load_sem.at[2 + k])
        for k in range(GROUPS * DIRS)]
    tok_load = pltpu.make_async_copy(
        tok_hbm, tok.at[:, pl.ds(pl.multiple_of(x * dx, 128), dx)], load_sem.at[0])
    cot_load = pltpu.make_async_copy(cot_hbm, cot, load_sem.at[1])
    for load in w_loads:
        load.start()
    tok_load.start()
    cot_load.start()

    barrier = pltpu.get_barrier_semaphore()
    for who in ring_to + [mate] + [peer(t) for t in range(1, peers)]:
        pl.semaphore_signal(
            barrier, inc=1, device_id=who, device_id_type=pl.DeviceIdType.MESH)
    pl.semaphore_wait(barrier, 3 + peers - 1)

    def remote(src, dst, ssem, rsem, who):
        return pltpu.make_async_remote_copy(
            src_ref=src, dst_ref=dst, send_sem=ssem, recv_sem=rsem,
            device_id=who, device_id_type=pl.DeviceIdType.MESH)

    def w_piece(g, d, pos, core, r):
        owner = chip_at(pos) * 2 + core
        return w_all.at[g * DIRS + d, pl.ds(pl.multiple_of(owner * S + r * sr, 16), sr)]

    def sem_at(g, d, h, r):
        return ((g * DIRS + d) * SPLIT + r) * n + h

    def sign(d):
        return 1 - 2 * d

    def ag_ring(g, d, h, r, back=0):
        piece = w_piece(g, d, p - sign(d) * (h + back), c, r)
        k = sem_at(g, d, h, r)
        return remote(piece, piece, ag_s.at[k], ag_r.at[k], ring_to[d])

    def ag_mate(g, d, h, r, core):
        piece = w_piece(g, d, p - sign(d) * h, core, r)
        k = sem_at(g, d, h, r)
        return remote(piece, piece, agp_s.at[k], agp_r.at[k], mate)

    def tok_copy(t, m):
        piece = tok.at[pl.ds(m * TILE, TILE), pl.ds(pl.multiple_of(x * dx, 128), dx)]
        k = (t - 1) * halves + m
        return remote(piece, piece, tok_s.at[k], tok_r.at[k], peer(t))

    def tok_in(t, m):
        source = lax.rem(x + peers - t, peers)
        piece = tok.at[pl.ds(m * TILE, TILE), pl.ds(pl.multiple_of(source * dx, 128), dx)]
        k = (t - 1) * halves + m
        return remote(piece, piece, tok_s.at[k], tok_r.at[k], peer(t))

    def ag_start(g):
        for r in range(SPLIT):
            for d in range(DIRS):
                ag_ring(g, d, 0, r).start()
        for r in range(SPLIT):
            for d in range(DIRS):
                ag_mate(g, d, 0, r, c).start()

    for load in w_loads:
        load.wait()
    ag_start(0)
    tok_load.wait()
    for m in range(halves):
        for t in range(1, peers):
            tok_copy(t, m).start()
    cot_load.wait()

    def wait_mates(g):
        @pl.loop(0, n)
        def _(h):
            for r in range(SPLIT):
                for d in range(DIRS):
                    ag_mate(g, d, h, r, 1 - c).wait_recv()

    def activate(g, u):
        m = lax.div(u, ntile)
        rsl = pl.ds(pl.multiple_of(m * TILE, TILE), TILE)
        csl = pl.ds(pl.multiple_of(g * gcols + lax.rem(u, ntile) * TILE, TILE), TILE)
        v = jnp.dot(tok[rsl, :], w_all[g * DIRS + lax.rem(u, ntile)],
                    preferred_element_type=F32)
        sq = v * v
        th = jnp.tanh(ROOT * v * (1.0 + 0.044715 * sq))
        half = 0.5 * (1.0 + th)
        hid[rsl, csl] = (v * half).astype(BF16)
        slope = half + 0.5 * v * (1.0 - th * th) * (ROOT * (1.0 + 3.0 * 0.044715 * sq))
        pg[rsl, csl] = (cot[rsl, csl].astype(F32) * slope).astype(BF16)

    def rs_owner(d, h):
        return chip_at(p - sign(d) * (h + 1))

    def slot(g, d, h):
        return (g * DIRS + d) * n + h

    def rs_ring(g, d, h, r):
        k = slot(g, d, h)
        at = pl.ds(r * sr, sr)
        j = sem_at(g, d, h, r)
        return remote(rsend.at[k, at], rrecv.at[k, at], rs_s.at[j], rs_r.at[j], ring_to[d])

    def rs_mate(g, d, h):
        k = slot(g, d, h)
        return remote(psend.at[k], precv.at[k], rsp_s.at[k], rsp_r.at[k], mate)

    def make_part(g, d, h):
        cols = g * gcols + d * qcols
        acc = part.at[g * DIRS + d]
        acc[...] = jnp.dot(
            tok_t[pl.ds(pl.multiple_of(rs_owner(d, h) * 2 * S, 16), 2 * S), :],
            pg[:, cols:cols + qcols], preferred_element_type=F32)
        psend[slot(g, d, h)] = acc[pl.ds(pl.multiple_of((1 - c) * S, 16), S), :].astype(BF16)
        rs_mate(g, d, h).start()

    def combine(g, h):
        for d in range(DIRS):
            rs_mate(g, d, h).wait_recv()
        for r in range(SPLIT):
            for d in range(DIRS):
                combine_piece(g, d, h, r)

    def combine_piece(g, d, h, r):
        k = slot(g, d, h)
        at = pl.ds(r * sr, sr)
        cols = g * gcols + d * qcols
        mine = part[g * DIRS + d, pl.ds(pl.multiple_of(c * S + r * sr, 16), sr), :]
        total = mine + precv[k, at].astype(F32)

        @pl.when(h == 0)
        def _():
            rsend[k, at] = total.astype(BF16)

        @pl.when(h > 0)
        def _():
            rs_ring(g, d, h - 1, r).wait_recv()
            full = (total + rrecv[k - 1, at].astype(F32)).astype(BF16)

            @pl.when(h < n - 1)
            def _():
                rsend[k, at] = full

            @pl.when(h == n - 1)
            def _():
                wg[at, cols:cols + qcols] = full

        @pl.when(h < n - 1)
        def _():
            rs_ring(g, d, h, r).start()

    strips = dx // 128
    others = (peers - 1) * strips

    def spread(count, i, steps):
        return lax.div(i * count, steps), lax.div((i + 1) * count, steps)

    def flip(m, col):
        at = pl.ds(pl.multiple_of(col, 128), 128)
        tok_t[at, m * TILE:(m + 1) * TILE] = tok[m * TILE:(m + 1) * TILE, at].T

    def flip_other(m, k):
        t = lax.div(k, strips) + 1
        flip(m, lax.rem(x + t, peers) * dx + lax.rem(k, strips) * 128)

    def await_tokens(m):
        for t in range(1, peers):
            tok_in(t, m).wait_recv()

    def x_block(owner, b):
        at = pl.ds(pl.multiple_of(owner * dx + b * xcols, 128), xcols)
        rows_of_w = jnp.concatenate(
            [w_all[k, at, :] for k in range(GROUPS * DIRS)], axis=1)
        return lax.dot_general(
            pg[...], rows_of_w, (((1,), (1,)), ((), ())),
            preferred_element_type=F32).astype(BF16)

    def x_copy(k):
        return remote(xsend.at[k], xrecv.at[k], x_s.at[k], x_r.at[k],
                      peer(lax.div(k, nb) + 1))

    away = (peers - 1) * nb

    done = n + REDUCE[-1]

    @pl.loop(0, done + n)
    def _(s):
        for g in range(GROUPS):
            h = s - g * AG_LAG

            @pl.when((h >= 0) & (h < n - 1))
            def _():
                for r in range(SPLIT):
                    for d in range(DIRS):
                        ag_ring(g, d, h, r, 1).wait_recv()

                        @pl.when(h < n - 2)
                        def _():
                            ag_ring(g, d, h + 1, r).start()

                        ag_mate(g, d, h + 1, r, c).start()

            if g + 1 < GROUPS:
                @pl.when(h == AG_LAG - 1)
                def _():
                    ag_start(g + 1)

        @pl.when(s < n - 1)
        def _():
            @pl.loop(*spread(strips, s, n - 1))
            def _(k):
                for m in range(halves):
                    flip(m, x * dx + k * 128)

        for g in range(GROUPS):
            i = s - n - READY[g]
            h = s - n - REDUCE[g]
            span = REDUCE[g] - READY[g]

            @pl.when((h >= 0) & (h < n))
            def _():
                combine(g, h)

            @pl.when((i >= 0) & (i < span))
            def _():
                @pl.when(i == 0)
                def _():
                    wait_mates(g)

                if g == 0:
                    for m in range(halves):
                        @pl.when(i == m * span // halves)
                        def _():
                            await_tokens(m)

                            @pl.loop(0, others)
                            def _(k):
                                flip_other(m, k)

                @pl.loop(*spread(units, i, span))
                def _(u):
                    activate(g, u)

            @pl.when((h >= -1) & (h < n - 1))
            def _():
                for d in range(DIRS):
                    make_part(g, d, h + 1)

        e = s - done

        @pl.when(e == 0)
        def _():
            @pl.loop(0, away)
            def _(k):
                t = lax.div(k, nb) + 1
                xsend[k] = x_block(lax.rem(x + t, peers), lax.rem(k, nb))
                x_copy(k).start()

        @pl.when((e >= 2) & (e < 6))
        def _():
            @pl.loop(*spread(nb, e - 2, 4))
            def _(b):
                xg[:, pl.ds(pl.multiple_of(b * xcols, 128), xcols)] = x_block(x, b)

        @pl.when((e >= 0) & (e < n))
        def _():
            for g in range(GROUPS):
                for d in range(DIRS):
                    for r in range(SPLIT):
                        ag_mate(g, d, e, r, c).wait_send()

                        @pl.when(e < n - 1)
                        def _():
                            ag_ring(g, d, e, r).wait_send()

        for g in range(GROUPS):
            h = s - n - REDUCE[g]

            @pl.when((h >= 2) & (h < n))
            def _():
                for d in range(DIRS):
                    rs_mate(g, d, h - 2).wait_send()
                    for r in range(SPLIT):
                        rs_ring(g, d, h - 2, r).wait_send()

    @pl.loop(0, nb)
    def _(b):
        at = pl.ds(pl.multiple_of(b * xcols, 128), xcols)
        total = xg[:, at].astype(F32)
        for t in range(1, peers):
            k = (t - 1) * nb + b
            x_copy(k).wait_recv()
            total = total + xrecv[k].astype(F32)
        xg[:, at] = total.astype(BF16)

    for g in range(GROUPS):
        for d in range(DIRS):
            for h in (n - 2, n - 1):
                rs_mate(g, d, h).wait_send()
            for r in range(SPLIT):
                rs_ring(g, d, n - 2, r).wait_send()

    @pl.loop(0, away)
    def _(k):
        x_copy(k).wait_send()

    for m in range(halves):
        for t in range(1, peers):
            tok_copy(t, m).wait_send()


def on_device(n_dp, peers, tokens, w_in, cotangent):
    n = n_dp // 2
    S, ff = w_in.shape
    rows, dx = tokens.shape
    D = dx * peers
    qcols = ff // (GROUPS * DIRS)
    xcols = min(384, dx)
    nx = (peers - 1) * (dx // xcols)
    slots = GROUPS * DIRS * n
    any_spec = pl.BlockSpec(memory_space=pltpu.HBM)
    vmem = pl.BlockSpec(memory_space=pltpu.VMEM)
    dma = pltpu.SemaphoreType.DMA
    halves = rows // TILE
    return pl.pallas_call(
        functools.partial(kernel, n, peers),
        out_shape=[
            pltpu.VMEM((rows, ff), BF16),
            pltpu.VMEM((rows, dx), BF16),
            pltpu.VMEM((S, ff), BF16),
        ],
        in_specs=[any_spec] * 3,
        out_specs=[vmem] * 3,
        scratch_shapes=[
            pltpu.VMEM((GROUPS * DIRS, D, qcols), BF16),
            pltpu.VMEM((rows, D), BF16),
            pltpu.VMEM((D, rows), BF16),
            pltpu.VMEM((rows, ff), BF16),
            pltpu.VMEM((rows, ff), BF16),
            pltpu.VMEM((GROUPS * DIRS, 2 * S, qcols), F32),
            pltpu.VMEM((slots, S, qcols), BF16),
            pltpu.VMEM((slots, S, qcols), BF16),
            pltpu.VMEM((slots, S, qcols), BF16),
            pltpu.VMEM((slots, S, qcols), BF16),
            pltpu.VMEM((nx, rows, xcols), BF16),
            pltpu.VMEM((nx, rows, xcols), BF16),
            dma((2 + GROUPS * DIRS,)),
            dma(((peers - 1) * halves,)), dma(((peers - 1) * halves,)),
            dma((slots * SPLIT,)), dma((slots * SPLIT,)),
            dma((slots * SPLIT,)), dma((slots * SPLIT,)),
            dma((slots * SPLIT,)), dma((slots * SPLIT,)), dma((slots,)), dma((slots,)),
            dma((nx,)), dma((nx,)),
        ],
        compiler_params=pltpu.CompilerParams(
            collective_id=0, has_side_effects=True,
            vmem_limit_bytes=60 * 1024 * 1024,
        ),
        cost_estimate=pl.CostEstimate(
            flops=6 * rows * D * ff, bytes_accessed=4 * (2 * rows * ff + rows * dx + S * ff),
            transcendentals=rows * ff),
    )(w_in, tokens, cotangent)


def solution(mesh):
    spec = P("dp", "tensor")
    return jax.shard_map(
        functools.partial(on_device, mesh.shape["dp"], mesh.shape["tensor"]),
        mesh=mesh, in_specs=(spec,) * 3, out_specs=(spec,) * 3, check_vma=False,
    )
```
